256 devices in a mesh: ctx: 64 (over x_lo, z, y), head: 4 (over x_hi, core).
Axes of the slice: x: 4 (x_hi: 2, x_lo: 2; x = x_hi * 2 + x_lo), y: 4, z: 8, core: 2. Of those that a mesh axis runs over, the one named last changes fastest.
Arguments:
- queries: bfloat16 [512, 8192], P('ctx', 'head'), may hold values from -32 to 32
- new_keys: bfloat16 [512, 512], P('ctx', 'head'), may hold values from -12 to 12
- new_values: bfloat16 [512, 512], P('ctx', 'head'), may hold values from -6 to 6
- cache_keys: bfloat16 [4, 4, 131072, 128], P('head', None, 'ctx'), may hold values from -6 to 6
- cache_values: bfloat16 [4, 4, 131072, 128], P('head', None, 'ctx'), may hold values from -6 to 6
- out_weight: bfloat16 [8192, 16384], P('head', 'ctx'), may hold values from -0.0625 to 0.0625
- context_lengths: int32 [4], replicated, may hold values from 1 to 131072, as said below
- turn_lengths: int32 [4], replicated, may hold values from 1 to 128, as said below
Outputs:
- projected: bfloat16 [512, 16384], P('head', 'ctx')
The draws below stay inside these ranges and needn't reach their ends.
Inputs may be any that keep to these rules, and one draw needn't show every extreme that they name: `context_lengths`: at least one rollout uses all 131072 cached positions. `turn_lengths`: at least one rollout uses all 128 new token slots.
All inputs are finite; a program needn't handle non-finite values.
Results may differ from the reference program's by a relative error of at most 0.019.
Values may be sent and summed in bfloat16 or wider, within the bound.
No kernel may reach another device: no remote copies, remote signals or barrier semaphores. Data moves between devices by JAX's collectives and lax.ppermute only.
A program may use at most 64 MiB of HBM per device.

```python
import jax
import jax.numpy as jnp
from jax import lax

D = 16384
HD = 128
QPK = 16
R = 4
NEW = 128
KVH = 4
QH = 64
TOKENS = 512
CAP = 131072


def shared_keys(key):
    drawn = jnp.clip(jax.random.normal(key, (KVH, R, CAP, HD), jnp.float32), -6.0, 6.0)
    return drawn


def draw_cache_keys(key, part):
    keys = shared_keys(key)
    return keys.astype(jnp.bfloat16)


def draw_queries(key, part):
    own_key = jax.random.fold_in(key, 11)
    return (3.0 * jnp.clip(jax.random.normal(own_key, (TOKENS, KVH * QPK * HD), jnp.float32), -6.0, 6.0)).astype(jnp.bfloat16)


def draw_context_lengths(key, part):
    key = jax.random.fold_in(key, 1)
    chosen_key = jax.random.fold_in(key, 2)
    lengths = jax.random.randint(key, (R,), 1, CAP + 1)
    longest = jax.random.randint(chosen_key, (), 0, R)
    return lengths.at[longest].set(CAP).astype(jnp.int32)


def draw_turn_lengths(key, part):
    key = jax.random.fold_in(key, 3)
    chosen_key = jax.random.fold_in(key, 4)
    lengths = jax.random.randint(key, (R,), 1, NEW + 1)
    longest = jax.random.randint(chosen_key, (), 0, R)
    return lengths.at[longest].set(NEW).astype(jnp.int32)


def levels(rng, dims, pieces, least, largest):
    def one(position, parts):
        heights = jax.random.uniform(jax.random.fold_in(jax.random.fold_in(rng, 6), position), (parts,), jnp.float32, least / len(pieces), largest / len(pieces))
        return jnp.repeat(jnp.exp(heights), dims[position] // parts).reshape((-1,) + (1,) * (len(dims) - position - 1))

    gain = one(*pieces[0])
    for cut in pieces[1:]:
        gain = gain * one(*cut)
    return gain


def centred(stream_key, dims, width, reach, pieces=(), kind=jnp.bfloat16):
    entries = jax.random.normal(stream_key, dims, jnp.float32) * width
    if len(pieces) > 0:
        entries = levels(stream_key, dims, pieces, -0.22, 0.18) * entries
    return jnp.clip(entries, min=-reach, max=reach).astype(kind)


def setup_inputs(seed: int = 0) -> dict:
    streams_of = jax.random.split(jax.random.key(seed), 9)
    return {
        "queries": draw_queries(jax.random.fold_in(streams_of[8], 71), 0),
        "new_keys": centred(streams_of[1], (TOKENS, KVH * HD), 2.0, 12.0, ((0, 64), (1, 4))),
        "new_values": centred(streams_of[2], (TOKENS, KVH * HD), 1.0, 6.0, ((0, 64), (1, 4))),
        "cache_keys": draw_cache_keys(jax.random.fold_in(streams_of[8], 71), 0),
        "cache_values": centred(streams_of[4], (KVH, R, CAP, HD), 1.0, 6.0, ((0, 4), (2, 64))),
        "out_weight": centred(streams_of[5], (QH * HD, D), (QH * HD) ** -0.5, 0.0625, ((0, 4), (1, 64))),
        "context_lengths": draw_context_lengths(jax.random.fold_in(streams_of[8], 71), 0),
        "turn_lengths": draw_turn_lengths(jax.random.fold_in(streams_of[8], 71), 0),
    }


FLOOR_SCORE = -1.0e30


def reference(queries, new_keys, new_values, cache_keys, cache_values, out_weight, context_lengths, turn_lengths):
    score_scale = HD ** -0.5
    query_all = queries.reshape(R, NEW, KVH, QPK, HD).transpose(2, 0, 1, 3, 4).reshape(KVH * R, NEW * QPK, HD)
    fresh_keys = new_keys.reshape(R, NEW, KVH, HD).transpose(2, 0, 1, 3).reshape(KVH * R, NEW, HD)
    fresh_values = new_values.reshape(R, NEW, KVH, HD).transpose(2, 0, 1, 3).reshape(KVH * R, NEW, HD)
    old_keys = cache_keys.reshape(KVH * R, CAP, HD)
    old_values = cache_values.reshape(KVH * R, CAP, HD)
    cache_lens = jnp.tile(context_lengths, KVH)
    fresh_lens = jnp.tile(turn_lengths, KVH)
    row_pos = jnp.arange(NEW * QPK, dtype=jnp.int32) // QPK
    key_pos = jnp.arange(NEW, dtype=jnp.int32)
    slot_ids = jnp.arange(CAP, dtype=jnp.int32)

    def attend(bundle):
        query_rows, key_old, value_old, key_new, value_new, cache_len, fresh_len = bundle
        keys = jnp.concatenate([key_old, key_new], axis=0)
        values = jnp.concatenate([value_old, value_new], axis=0)
        scores = jnp.dot(query_rows, keys.T, preferred_element_type=jnp.float32) * score_scale
        seen_old = jnp.broadcast_to((slot_ids < cache_len)[None, :], (NEW * QPK, CAP))
        seen_new = (key_pos[None, :] <= row_pos[:, None]) & (key_pos[None, :] < fresh_len)
        visible = jnp.concatenate([seen_old, seen_new], axis=1)
        scores = jnp.where(visible, scores, FLOOR_SCORE)
        row_top = jnp.max(scores, axis=1)
        weights = jnp.where(visible, jnp.exp(scores - row_top[:, None]), 0.0)
        denominator = jnp.sum(weights, axis=1)
        numerator = jnp.dot(weights.astype(jnp.bfloat16), values, preferred_element_type=jnp.float32)
        return (numerator / denominator[:, None]).astype(jnp.bfloat16)

    attended = lax.map(attend, (query_all, old_keys, old_values, fresh_keys, fresh_values, cache_lens, fresh_lens))
    attended = attended.reshape(KVH, R, NEW, QPK, HD).transpose(1, 2, 0, 3, 4).reshape(TOKENS, KVH * QPK * HD)
    return jnp.dot(attended, out_weight, preferred_element_type=jnp.float32).astype(jnp.bfloat16)
```

```python
import functools

import jax
import jax.numpy as jnp
from jax import lax
from jax.experimental import pallas as pl
from jax.experimental.pallas import tpu as pltpu
from jax.sharding import Mesh
from jax.sharding import PartitionSpec as P

FLOOR = -(2.0**99)
LOG2E = 1.4426950408889634
BF = jnp.bfloat16
F32 = jnp.float32
AUX = 16
XL, NZ, NY, XH, CORE = 2, 8, 4, 2, 2
CTX = ("xl", "z", "y")
HEAD = ("xh", "core")
VMEM_LIMIT = 60 * 2**20


def dot_t(a, b):
    return lax.dot_general(a, b, (((1,), (1,)), ((), ())), preferred_element_type=F32)


def attend_kernel(sub, sc_ref, q_ref, k_ref, v_ref, nk_ref, nv_ref, o_ref, n_s, l_s, m_s):
    r = pl.program_id(0)
    nb, brow, hd = q_ref.shape
    rows = nb * brow
    slots = k_ref.shape[1]
    nvis = sc_ref[r]
    qf = q_ref[...].reshape(rows, hd).astype(F32) * (hd**-0.5 * LOG2E)
    hi = qf.astype(BF)
    lo = (qf - hi.astype(F32)).astype(BF)
    qq = jnp.concatenate([hi, lo], axis=1)

    def cached(masked):
        k = k_ref[0]
        v = v_ref[0]
        kk = jnp.concatenate([k, k], axis=1)
        vv = jnp.concatenate([v, jnp.ones_like(v)], axis=1)
        for i in range(rows // sub):
            sl = slice(i * sub, (i + 1) * sub)
            s = dot_t(qq[sl], kk)
            if masked:
                col = lax.broadcasted_iota(jnp.int32, (1, slots), 1)
                s = jnp.where(col < nvis, s, FLOOR)
            m = jnp.max(s, axis=1, keepdims=True).astype(BF).astype(F32)
            p = jnp.exp2(s - m).astype(BF)
            pv = jnp.dot(p, vv, preferred_element_type=F32)
            n_s[sl] = pv[:, :hd]
            l_s[sl] = pv[:, hd:]
            m_s[sl] = jnp.broadcast_to(m, (sub, hd))

    pl.when(nvis >= slots)(lambda: cached(False))
    pl.when((nvis < slots) & (nvis > 0))(lambda: cached(True))

    @pl.when(nvis <= 0)
    def _():
        n_s[...] = jnp.zeros_like(n_s)
        l_s[...] = jnp.zeros_like(l_s)
        m_s[...] = jnp.full_like(m_s, FLOOR)

    @pl.when(r == sc_ref[4])
    def _():
        nk = nk_ref[...]
        nv = nv_ref[...]
        s = dot_t(qq, jnp.concatenate([nk, nk], axis=1))
        row = lax.broadcasted_iota(jnp.int32, s.shape, 0)
        col = lax.broadcasted_iota(jnp.int32, s.shape, 1)
        tok = (row // brow) * sc_ref[8] + sc_ref[7] + row % sc_ref[9]
        j = sc_ref[5] + col
        seen = (col < sc_ref[9]) & (j <= tok) & (j < sc_ref[6])
        s = jnp.where(seen, s, FLOOR)
        mo = m_s[...]
        mn = jnp.maximum(mo, jnp.max(s, axis=1, keepdims=True)).astype(BF).astype(F32)
        a = jnp.exp2(mo - mn)
        p = jnp.where(seen, jnp.exp2(s - mn), 0.0).astype(BF)
        pv = jnp.dot(p, jnp.concatenate([nv, jnp.ones_like(nv)], axis=1), preferred_element_type=F32)
        n_s[...] = n_s[...] * a + pv[:, :hd]
        l_s[...] = l_s[...] * a + pv[:, hd:]
        m_s[...] = mn

    lane = lax.broadcasted_iota(jnp.int32, (brow, hd), 1)
    for b in range(nb):
        sl = slice(b * brow, (b + 1) * brow)
        o_ref[b, :brow, :] = n_s[sl].astype(BF)
        total = l_s[sl]
        head = total.astype(BF).astype(F32)
        aux = jnp.where(lane == 0, m_s[sl], jnp.where(lane == 1, head, total - head))
        o_ref[b, brow:, :] = aux.T[:AUX].astype(BF)


def attend(sc, q, k, v, nk, nv, sub=256):
    nblk, brow, hd = q.shape
    roll, slots = k.shape[0], k.shape[1]
    nb = nblk // roll
    rows = nb * brow
    return pl.pallas_call(
        functools.partial(attend_kernel, sub),
        grid_spec=pltpu.PrefetchScalarGridSpec(
            num_scalar_prefetch=1,
            grid=(roll,),
            in_specs=[
                pl.BlockSpec((nb, brow, hd), lambda r, s: (r, 0, 0)),
                pl.BlockSpec((1, slots, hd), lambda r, s: (r, 0, 0)),
                pl.BlockSpec((1, slots, hd), lambda r, s: (r, 0, 0)),
                pl.BlockSpec(nk.shape, lambda r, s: (0, 0)),
                pl.BlockSpec(nv.shape, lambda r, s: (0, 0)),
            ],
            out_specs=pl.BlockSpec((nb, brow + AUX, hd), lambda r, s: (r, 0, 0)),
            scratch_shapes=[pltpu.VMEM((rows, hd), F32)] * 3,
        ),
        out_shape=jax.ShapeDtypeStruct((nblk, brow + AUX, hd), BF),
        compiler_params=pltpu.CompilerParams(vmem_limit_bytes=VMEM_LIMIT),
        cost_estimate=pl.CostEstimate(
            flops=8 * roll * rows * slots * hd,
            bytes_accessed=4 * roll * slots * hd,
            transcendentals=roll * rows * slots,
        ),
        name="attend",
    )(sc, q, k, v, nk, nv)


def weights_of(auxs):
    tops = [a[0:1] for a in auxs]
    sums = [a[1:2] + a[2:3] for a in auxs]
    top = functools.reduce(jnp.maximum, tops)
    ws = [jnp.exp2(t - top) for t in tops]
    total = functools.reduce(jnp.add, [w * s for w, s in zip(ws, sums)])
    return top, ws, total


def columns(rows_list):
    n = len(rows_list)
    lanes = rows_list[0].shape[1]
    pad = jnp.zeros((lanes - n, lanes), F32)
    return jnp.concatenate(list(rows_list) + [pad], axis=0).T


def merge_kernel(a_ref, b_ref, c_ref, d_ref, o_ref):
    parts = (a_ref, b_ref, c_ref, d_ref)
    nb = o_ref.shape[0]
    brow = o_ref.shape[1] - AUX
    for b in range(nb):
        top, ws, total = weights_of([p[b, brow:, :].astype(F32) for p in parts])
        cols = columns(ws)
        acc = 0.0
        for i, p in enumerate(parts):
            acc = acc + cols[:, i : i + 1] * p[b, :brow, :].astype(F32)
        o_ref[b, :brow, :] = acc.astype(BF)
        head = total.astype(BF).astype(F32)
        aux = jnp.concatenate([top, head, total - head, jnp.zeros((AUX - 3, total.shape[1]), F32)], axis=0)
        o_ref[b, brow:, :] = aux.astype(BF)


def merge(parts, roll):
    nblk, prow, hd = parts[0].shape
    spec = pl.BlockSpec((nblk // roll, prow, hd), lambda r: (r, 0, 0))
    return pl.pallas_call(
        merge_kernel,
        grid=(roll,),
        in_specs=[spec] * len(parts),
        out_specs=spec,
        out_shape=jax.ShapeDtypeStruct(parts[0].shape, BF),
        name="merge",
    )(*parts)


def finish_kernel(tok, x_ref, o_ref):
    n, prow, hd = x_ref.shape
    brow = prow - AUX
    _, ws, total = weights_of([x_ref[i, brow:, :].astype(F32) for i in range(n)])
    inv = 1.0 / total
    cols = columns([w * inv for w in ws])
    acc = 0.0
    for i in range(n):
        acc = acc + cols[:, i : i + 1] * x_ref[i, :brow, :].astype(F32)
    rows = jnp.concatenate([acc[g * tok : (g + 1) * tok] for g in range(brow // tok)], axis=1)
    pair = jnp.concatenate([rows, rows], axis=0).astype(BF)
    step = 2 * tok
    for c in range(n // 2):
        o_ref[c * step : (c + 1) * step, :] = pair


def finish(x, tok):
    n, prow, hd = x.shape
    groups = (prow - AUX) // tok
    return pl.pallas_call(
        functools.partial(finish_kernel, tok),
        out_shape=jax.ShapeDtypeStruct((n * tok, groups * hd), BF),
        name="finish",
    )(x)


def shift(x, k):
    return lax.ppermute(x, "y", [(i, (i + k) % NY) for i in range(NY)])


def on_device(queries, new_keys, new_values, cache_keys, cache_values, out_weight, context_lengths, turn_lengths):
    tok, q_width = queries.shape
    hd = cache_keys.shape[3]
    groups = q_width // hd
    roll, slots = cache_keys.shape[1], cache_keys.shape[2]
    ctx = lax.axis_index(CTX)
    y = lax.axis_index("y")
    blocks = XL * NZ
    per_roll = blocks * NY // roll
    brow = groups * tok
    plane = ("xl", "z")

    rows = queries.reshape(tok, groups, hd).transpose(1, 0, 2).reshape(1, brow, hd)
    q0 = lax.all_to_all(jnp.broadcast_to(rows, (blocks, brow, hd)), plane, 0, 0, tiled=True)
    qs = {0: q0}
    for k in (1, 3, 2):
        qs[k] = shift(q0, k)

    nvis = jnp.clip(context_lengths - ctx * slots, 0, slots)
    own = ctx // per_roll
    own_len = lax.dynamic_index_in_dim(turn_lengths, own, 0, keepdims=False)
    first = (ctx % per_roll) * tok
    nk = jnp.pad(new_keys, ((0, hd - tok), (0, 0)))
    nv = jnp.pad(new_values, ((0, hd - tok), (0, 0)))

    parts = []
    for k in (0, 1, 3, 2):
        off = ((y - k) % NY) * tok
        sc = jnp.concatenate(
            [nvis, jnp.stack([own, first, own_len, off, jnp.int32(NY * tok), jnp.int32(tok)])]
        ).astype(jnp.int32)
        part = attend(sc, qs[k], cache_keys[0], cache_values[0], nk, nv)
        parts.append(part if k == 0 else shift(part, -k))

    merged = merge(parts, roll)
    gathered = lax.all_to_all(merged, plane, 0, 0, tiled=True)
    copies = finish(gathered, tok)
    a0 = lax.all_to_all(copies, plane, 0, 0, tiled=True)
    outs = []
    for k in (0, 1, 3, 2):
        a = a0 if k == 0 else shift(a0, k)
        outs.append((k, jnp.dot(a, out_weight, preferred_element_type=F32).astype(BF)))
    outs = [o for _, o in sorted(outs, key=lambda t: t[0])]
    width = out_weight.shape[1]
    rb = blocks * tok // roll
    mine = jnp.stack([o.reshape(roll, rb, width) for o in outs], axis=1)
    got = lax.all_to_all(mine, HEAD, 0, 0, tiled=True)
    total = jnp.sum(got.astype(F32), axis=0).astype(BF)
    total = total.reshape(NY, rb // tok, tok, width)
    placed = [
        lax.dynamic_index_in_dim(total, (y - j) % NY, 0, keepdims=False) for j in range(NY)
    ]
    return jnp.stack(placed, axis=1).reshape(NY * rb, width)


def solution(mesh):
    fine = Mesh(mesh.devices.reshape(XL, NZ, NY, XH, CORE), ("xl", "z", "y", "xh", "core"))
    in_specs = (
        P(CTX, HEAD),
        P(CTX, HEAD),
        P(CTX, HEAD),
        P(HEAD, None, CTX, None),
        P(HEAD, None, CTX, None),
        P(HEAD, CTX),
        P(),
        P(),
    )
    return jax.shard_map(
        on_device, mesh=fine, in_specs=in_specs, out_specs=P(HEAD, CTX), check_vma=False
    )
```

```python
import functools

import jax
import jax.numpy as jnp
from jax import lax
from jax.experimental import pallas as pl
from jax.experimental.pallas import tpu as pltpu
from jax.sharding import Mesh
from jax.sharding import PartitionSpec as P

FLOOR = -(2.0**99)
LOG2E = 1.4426950408889634
BF = jnp.bfloat16
F32 = jnp.float32
AUX = 16
XL, NZ, NY, XH, CORE = 2, 8, 4, 2, 2
VM = pl.BlockSpec(memory_space=pltpu.VMEM)
ANY = pl.BlockSpec(memory_space=pl.ANY)
CTX = ("xl", "z", "y")
HEAD = ("xh", "core")
ATTEND_VMEM = 36 * 2**20
LEAD_VMEM = 60 * 2**20


def dot_t(a, b):
    return lax.dot_general(a, b, (((1,), (1,)), ((), ())), preferred_element_type=F32)


def attend_kernel(hop, sub, span, n_after, lead, cl_hbm, tl_hbm, q_ref, k_in, v_in, nk_ref, nv_ref, *rest):
    o_ref, token, cl_ref, tl_ref, n_s, l_s, m_s, sems = rest[n_after : n_after + 8]
    k_ref, v_ref = rest[n_after + 8 :] if lead else (k_in, v_in)
    token[...] = jnp.zeros_like(token)
    nblk, brow, hd = q_ref.shape
    roll, slots = k_in.shape[0], k_in.shape[1]
    nb = nblk // roll
    rows = nb * brow
    tok = nk_ref.shape[0]
    small = [
        pltpu.make_async_copy(cl_hbm, cl_ref, sems.at[0]),
        pltpu.make_async_copy(tl_hbm, tl_ref, sems.at[1]),
    ]
    for c in small:
        c.start()

    def load(r):
        slot = r - span[0]
        return (
            pltpu.make_async_copy(k_in.at[r], k_ref.at[slot], sems.at[2 + 2 * slot]),
            pltpu.make_async_copy(v_in.at[r], v_ref.at[slot], sems.at[3 + 2 * slot]),
        )

    if lead:
        for r in range(*span):
            for c in load(r):
                c.start()
    for c in small:
        c.wait()
    y = lax.axis_index("y")
    ctx = (lax.axis_index("xl") * NZ + lax.axis_index("z")) * NY + y
    per_roll = nblk * NY // roll
    own = lax.div(ctx, per_roll)
    first = lax.rem(ctx, per_roll) * tok
    off = lax.rem(y - hop + NY, NY) * tok
    lane = lax.broadcasted_iota(jnp.int32, (brow, hd), 1)

    def one(r, carry):
        base = r * nb
        kept = r
        if lead:
            for c in load(r):
                c.wait()
            kept = r - span[0]
        nvis = jnp.clip(cl_ref[r] - ctx * slots, 0, slots)
        qf = q_ref[pl.ds(base, nb)].reshape(rows, hd).astype(F32) * (hd**-0.5 * LOG2E)
        hi = qf.astype(BF)
        lo = (qf - hi.astype(F32)).astype(BF)
        qq = jnp.concatenate([hi, lo], axis=1)

        def cached(masked):
            k = k_ref[kept]
            v = v_ref[kept]
            kk = jnp.concatenate([k, k], axis=1)
            vv = jnp.concatenate([v, jnp.ones_like(v)], axis=1)
            n = rows // sub
            cut = [slice(i * sub, (i + 1) * sub) for i in range(n)]
            ahead = dot_t(qq[cut[0]], kk)
            for i in range(n):
                s = ahead
                if i + 1 < n:
                    ahead = dot_t(qq[cut[i + 1]], kk)
                if masked:
                    col = lax.broadcasted_iota(jnp.int32, (1, slots), 1)
                    s = jnp.where(col < nvis, s, FLOOR)
                m = jnp.max(s, axis=1, keepdims=True).astype(BF).astype(F32)
                p = jnp.exp2(s - m).astype(BF)
                pv = jnp.dot(p, vv, preferred_element_type=F32)
                n_s[cut[i]] = pv[:, :hd]
                l_s[cut[i]] = pv[:, hd:]
                m_s[cut[i]] = jnp.broadcast_to(m, (sub, hd))

        pl.when(nvis >= slots)(lambda: cached(False))
        pl.when((nvis < slots) & (nvis > 0))(lambda: cached(True))

        @pl.when(nvis <= 0)
        def _():
            n_s[...] = jnp.zeros_like(n_s)
            l_s[...] = jnp.zeros_like(l_s)
            m_s[...] = jnp.full_like(m_s, FLOOR)

        @pl.when(r == own)
        def _():
            pad = jnp.zeros((hd - tok, hd), F32)
            nk = jnp.concatenate([nk_ref[...].astype(F32), pad], axis=0).astype(BF)
            nv = jnp.concatenate([nv_ref[...].astype(F32), pad], axis=0).astype(BF)
            s = dot_t(qq, jnp.concatenate([nk, nk], axis=1))
            row = lax.broadcasted_iota(jnp.int32, s.shape, 0)
            col = lax.broadcasted_iota(jnp.int32, s.shape, 1)
            t = (row // brow) * (NY * tok) + off + row % tok
            j = first + col
            seen = (col < tok) & (j <= t) & (j < tl_ref[r])
            s = jnp.where(seen, s, FLOOR)
            mo = m_s[...]
            mn = jnp.maximum(mo, jnp.max(s, axis=1, keepdims=True)).astype(BF).astype(F32)
            a = jnp.exp2(mo - mn)
            p = jnp.where(seen, jnp.exp2(s - mn), 0.0).astype(BF)
            pv = jnp.dot(p, jnp.concatenate([nv, jnp.ones_like(nv)], axis=1), preferred_element_type=F32)
            n_s[...] = n_s[...] * a + pv[:, :hd]
            l_s[...] = l_s[...] * a + pv[:, hd:]
            m_s[...] = mn

        for b in range(nb):
            sl = slice(b * brow, (b + 1) * brow)
            o_ref[base - span[0] * nb + b, :brow, :] = n_s[sl].astype(BF)
            total = l_s[sl]
            head = total.astype(BF).astype(F32)
            aux = jnp.where(lane == 0, m_s[sl], jnp.where(lane == 1, head, total - head))
            o_ref[base - span[0] * nb + b, brow:, :] = aux.T[:AUX].astype(BF)
        return carry

    lax.fori_loop(span[0], span[1], one, 0)


def attend(hop, cl, tl, q, k, v, nk, nv, after=(), span=None, lead=False, sub=256):
    nblk, brow, hd = q.shape
    roll, slots = k.shape[0], k.shape[1]
    span = span or (0, roll)
    rows = nblk // roll * brow
    n = span[1] - span[0]
    return pl.pallas_call(
        functools.partial(attend_kernel, hop, sub, span, len(after), lead),
        in_specs=[ANY, ANY, VM] + [ANY if lead else VM] * 2 + [VM, VM] + [ANY] * len(after),
        out_specs=[VM, VM],
        out_shape=[
            jax.ShapeDtypeStruct((nblk // roll * n, brow + AUX, hd), BF),
            jax.ShapeDtypeStruct((8, 128), F32),
        ],
        scratch_shapes=[pltpu.SMEM((roll,), jnp.int32)] * 2
        + [pltpu.VMEM((rows, hd), F32)] * 3
        + [pltpu.SemaphoreType.DMA((2 + 2 * n,))]
        + ([pltpu.VMEM((n, slots, hd), BF)] * 2 if lead else []),
        compiler_params=pltpu.CompilerParams(vmem_limit_bytes=LEAD_VMEM if lead else ATTEND_VMEM),
        cost_estimate=pl.CostEstimate(
            flops=8 * n * rows * slots * hd,
            bytes_accessed=4 * n * slots * hd,
            transcendentals=n * rows * slots,
        ),
        name="attend",
    )(cl, tl, q, k, v, nk, nv, *after)


def weights_of(auxs):
    tops = [a[0:1] for a in auxs]
    sums = [a[1:2] + a[2:3] for a in auxs]
    top = functools.reduce(jnp.maximum, tops)
    ws = [jnp.exp2(t - top) for t in tops]
    total = functools.reduce(jnp.add, [w * s for w, s in zip(ws, sums)])
    return top, ws, total


def columns(rows_list):
    n = len(rows_list)
    lanes = rows_list[0].shape[1]
    pad = jnp.zeros((lanes - n, lanes), F32)
    return jnp.concatenate(list(rows_list) + [pad], axis=0).T


def merge_kernel(lo_ref, hi_ref, b_ref, c_ref, d_ref, w_ref, o_ref, first_ref, second_ref):
    half = first_ref.shape[0]
    first_ref[...] = w_ref[:half]
    second_ref[...] = w_ref[half:]
    nb, prow, lanes = o_ref.shape
    brow = prow - AUX
    cut = lo_ref.shape[0]
    for b in range(nb):
        own = (lo_ref, b) if b < cut else (hi_ref, b - cut)
        parts = (own, (b_ref, b), (c_ref, b), (d_ref, b))
        top, ws, total = weights_of([p[i, brow:, :].astype(F32) for p, i in parts])
        cols = columns(ws)
        acc = 0.0
        for n, (p, i) in enumerate(parts):
            acc = acc + cols[:, n : n + 1] * p[i, :brow, :].astype(F32)
        o_ref[b, :brow, :] = acc.astype(BF)
        head = total.astype(BF).astype(F32)
        aux = jnp.concatenate([top, head, total - head, jnp.zeros((AUX - 3, lanes), F32)], axis=0)
        o_ref[b, brow:, :] = aux.astype(BF)


def merge(parts, w):
    half = jax.ShapeDtypeStruct((w.shape[0] // 2, w.shape[1]), w.dtype)
    return pl.pallas_call(
        merge_kernel,
        in_specs=[VM] * (len(parts) + 1),
        out_specs=(VM, VM, VM),
        out_shape=(jax.ShapeDtypeStruct(parts[-1].shape, BF), half, half),
        name="merge",
    )(*parts, w)


def finish_kernel(tok, x_ref, *rest):
    o_ref = rest[-1]
    n, prow, _ = x_ref.shape
    brow = prow - AUX
    _, ws, total = weights_of([x_ref[i, brow:, :].astype(F32) for i in range(n)])
    inv = 1.0 / total
    cols = columns([w * inv for w in ws])
    acc = 0.0
    for i in range(n):
        acc = acc + cols[:, i : i + 1] * x_ref[i, :brow, :].astype(F32)
    rows = jnp.concatenate([acc[g * tok : (g + 1) * tok] for g in range(brow // tok)], axis=1)
    pair = jnp.concatenate([rows, rows], axis=0).astype(BF)
    step = 2 * tok
    for c in range(n // 2):
        o_ref[c * step : (c + 1) * step, :] = pair


def finish(x, tok, after):
    n, prow, hd = x.shape
    width = (prow - AUX) // tok * hd
    return pl.pallas_call(
        functools.partial(finish_kernel, tok),
        in_specs=[VM] + [ANY] * len(after),
        out_specs=VM,
        out_shape=jax.ShapeDtypeStruct((n * tok, width), BF),
        name="finish",
    )(x, *after)


def project_kernel(a_ref, w_ref, *rest):
    o_ref = rest[-1]
    half = w_ref.shape[0] // 2
    y = lax.axis_index("y")
    pieces = [(w_ref.at[:half], w_ref.at[half:])] + [rest[2 * i : 2 * i + 2] for i in range(NY - 1)]
    for k, (top, low) in enumerate(pieces):
        out = jnp.dot(a_ref[:, :half], top[...], preferred_element_type=F32)
        out = out + jnp.dot(a_ref[:, half:], low[...], preferred_element_type=F32)
        o_ref[lax.rem(y - k + NY, NY)] = out.astype(BF)


def project(a, w, others):
    return pl.pallas_call(
        project_kernel,
        in_specs=[VM] * (2 + len(others)),
        out_specs=VM,
        out_shape=jax.ShapeDtypeStruct((NY, a.shape[0], w.shape[1]), BF),
        name="project",
    )(a, w, *others)


def shift(x, k):
    return lax.ppermute(x, "y", [(i, (i + k) % NY) for i in range(NY)])


def on_device(queries, new_keys, new_values, cache_keys, cache_values, out_weight, context_lengths, turn_lengths):
    tok, q_width = queries.shape
    hd = cache_keys.shape[3]
    groups = q_width // hd
    roll = cache_keys.shape[1]
    blocks = XL * NZ
    brow = groups * tok
    plane = ("xl", "z")
    hops = (0, 2, 1, 3)

    rows = queries.reshape(tok, groups, hd).transpose(1, 0, 2).reshape(1, brow, hd)
    half = q_width // 2
    up1, low3 = shift(out_weight[:half], 1), shift(out_weight[half:], 3)
    q0 = lax.all_to_all(jnp.broadcast_to(rows, (blocks, brow, hd)), plane, 0, 0, tiled=True)
    qs = {k: shift(q0, k) for k in hops[1:]}
    lens = (context_lengths, turn_lengths)
    kv = (cache_keys[0], cache_values[0], new_keys, new_values)

    lo, token = attend(0, *lens, q0, *kv, after=(up1, low3), span=(0, roll // 2), lead=True)
    parts = {}
    for k in hops[1:]:
        part, _ = attend(k, *lens, qs[k], *kv, after=(token,))
        parts[k] = shift(part, -k)
    hi, _ = attend(0, *lens, q0, *kv, after=(token,), span=(roll // 2, roll))
    merged, top, low = merge([lo, hi] + [parts[k] for k in hops[1:]], out_weight)

    up3, low1 = shift(top, 3), shift(low, 1)
    gathered = lax.all_to_all(merged, plane, 0, 0, tiled=True)
    copies = finish(gathered, tok, (up3, low1))
    up2, low2 = shift(up1, 1), shift(low3, 3)
    attended = lax.all_to_all(copies, plane, 0, 0, tiled=True).reshape(blocks * tok, q_width)
    width = out_weight.shape[1]
    rb = blocks * tok // roll
    mine = project(attended, out_weight, (up1, low1, up2, low2, up3, low3))
    got = lax.all_to_all(mine.reshape(NY * roll, rb, width), ("y",) + HEAD, 0, 0, tiled=True)
    total = jnp.sum(got.reshape(NY, roll, rb // tok, tok, width).astype(F32), axis=1)
    return total.astype(BF).transpose(1, 0, 2, 3).reshape(NY * rb, width)


def solution(mesh):
    fine = Mesh(mesh.devices.reshape(XL, NZ, NY, XH, CORE), ("xl", "z", "y", "xh", "core"))
    in_specs = (
        P(CTX, HEAD),
        P(CTX, HEAD),
        P(CTX, HEAD),
        P(HEAD, None, CTX, None),
        P(HEAD, None, CTX, None),
        P(HEAD, CTX),
        P(),
        P(),
    )
    return jax.shard_map(
        on_device, mesh=fine, in_specs=in_specs, out_specs=P(HEAD, CTX), check_vma=False
    )
```

```python
import functools

import jax
import jax.numpy as jnp
from jax import lax
from jax.experimental import pallas as pl
from jax.experimental.pallas import tpu as pltpu
from jax.sharding import Mesh
from jax.sharding import PartitionSpec as P

FLOOR = -(2.0**99)
LOG2E = 1.4426950408889634
BF = jnp.bfloat16
F32 = jnp.float32
AUX = 16
XL, NZ, NY, XH, CORE = 2, 8, 4, 2, 2
VM = pl.BlockSpec(memory_space=pltpu.VMEM)
ANY = pl.BlockSpec(memory_space=pl.ANY)
CTX = ("xl", "z", "y")
HEAD = ("xh", "core")
ATTEND_VMEM = 36 * 2**20
SMALL_VMEM = 16 * 2**20


def dot_t(a, b):
    return lax.dot_general(a, b, (((1,), (1,)), ((), ())), preferred_element_type=F32)


def prepare_kernel(k_in, v_in, nk_in, nv_in, k_out, v_out, nk_out, nv_out, sems):
    pairs = ((k_in, k_out), (v_in, v_out), (nk_in, nk_out), (nv_in, nv_out))
    copies = [pltpu.make_async_copy(a, b, sems.at[i]) for i, (a, b) in enumerate(pairs)]
    for c in copies:
        c.start()
    for c in copies:
        c.wait()


def prepare(*given):
    return pl.pallas_call(
        prepare_kernel,
        in_specs=[ANY] * len(given),
        out_specs=[VM] * len(given),
        out_shape=[jax.ShapeDtypeStruct(a.shape, a.dtype) for a in given],
        scratch_shapes=[pltpu.SemaphoreType.DMA((len(given),))],
        compiler_params=pltpu.CompilerParams(vmem_limit_bytes=SMALL_VMEM),
        name="prepare",
    )(*given)


def attend_kernel(hop, sub, tk, span, n_after, cl_hbm, tl_hbm, q_ref, k_ref, v_ref, nk_ref, nv_ref, *rest):
    o_ref, token, cl_ref, tl_ref, n_s, l_s, m_s, sems = rest[n_after : n_after + 8]
    token[...] = jnp.zeros_like(token)
    blocks, brow, hd = q_ref.shape
    roll, slots = k_ref.shape[0], k_ref.shape[1]
    nb = XL * NZ // roll
    nblk = nb * roll
    held = 0 if blocks == nblk else span[0]
    rows = nb * brow
    tok = nk_ref.shape[0]
    small = [
        pltpu.make_async_copy(cl_hbm, cl_ref, sems.at[0]),
        pltpu.make_async_copy(tl_hbm, tl_ref, sems.at[1]),
    ]
    for c in small:
        c.start()
    for c in small:
        c.wait()
    y = lax.axis_index("y")
    ctx = (lax.axis_index("xl") * NZ + lax.axis_index("z")) * NY + y
    per_roll = nblk * NY // roll
    own = lax.div(ctx, per_roll)
    first = lax.rem(ctx, per_roll) * tok
    off = lax.rem(y - hop + NY, NY) * tok
    lane = lax.broadcasted_iota(jnp.int32, (brow, hd), 1)

    n_roll = span[1] - span[0]
    seen_slots = [jnp.clip(cl_ref[r] - ctx * slots, 0, slots) for r in range(*span)]
    slot_of = lax.broadcasted_iota(jnp.int32, (1, slots), 1)
    tiles = [slice(t * tk, (t + 1) * tk) for t in range(slots // tk)]
    subs = [(r, i) for r in range(*span) for i in range(rows // sub)]

    def split(base, count):
        qf = q_ref[pl.ds(base, count)].reshape(count * brow, hd).astype(F32) * (hd**-0.5 * LOG2E)
        hi = qf.astype(BF)
        lo = (qf - hi.astype(F32)).astype(BF)
        return jnp.concatenate([hi, lo], axis=1)

    def score(qq, r, t):
        k = k_ref[r, tiles[t], :]
        s = dot_t(qq, jnp.concatenate([k, k], axis=1))
        return jnp.where(slot_of[:, tiles[t]] < seen_slots[r - span[0]], s, FLOOR)

    def peak(s, top):
        for c in range(tk // hd):
            part = s[:, c * hd : (c + 1) * hd]
            top = part if top is None else jnp.maximum(top, part)
        return top

    def queries_of(step):
        r, i = step
        per = sub // brow
        return split((r - held) * nb + i * per, per)

    qq = queries_of(subs[0])
    ahead, top = [], None
    for t in range(len(tiles)):
        ahead.append(score(qq, subs[0][0], t))
        top = peak(ahead[-1], top)
    for x, (r, i) in enumerate(subs):
        now, ahead = ahead, []
        m = jnp.max(top, axis=1, keepdims=True).astype(BF).astype(F32)
        top = None
        pv = None
        more = x + 1 < len(subs)
        if more:
            qq = queries_of(subs[x + 1])
        for t in range(len(tiles)):
            if more:
                ahead.append(score(qq, subs[x + 1][0], t))
            p = jnp.exp2(now[t] - m).astype(BF)
            v = v_ref[r, tiles[t], :]
            add = jnp.dot(p, jnp.concatenate([v, jnp.ones_like(v)], axis=1), preferred_element_type=F32)
            pv = add if pv is None else pv + add
            if more:
                top = peak(ahead[-1], top)
        at = (r - span[0], slice(i * sub, (i + 1) * sub))
        some = seen_slots[r - span[0]] > 0
        n_s[at] = jnp.where(some, pv[:, :hd], 0.0)
        l_s[at] = jnp.where(some, pv[:, hd:], 0.0)
        m_s[at] = jnp.broadcast_to(m, (sub, hd))

    @pl.when((own >= span[0]) & (own < span[1]))
    def _():
        pad = jnp.zeros((hd - tok, hd), F32)
        nk = jnp.concatenate([nk_ref[...].astype(F32), pad], axis=0).astype(BF)
        nv = jnp.concatenate([nv_ref[...].astype(F32), pad], axis=0).astype(BF)
        s = dot_t(split((own - held) * nb, nb), jnp.concatenate([nk, nk], axis=1))
        row = lax.broadcasted_iota(jnp.int32, s.shape, 0)
        col = lax.broadcasted_iota(jnp.int32, s.shape, 1)
        t = (row // brow) * (NY * tok) + off + row % tok
        j = first + col
        seen = (col < tok) & (j <= t) & (j < tl_ref[own])
        s = jnp.where(seen, s, FLOOR)
        at = own - span[0]
        mo = m_s[at]
        mn = jnp.maximum(mo, jnp.max(s, axis=1, keepdims=True)).astype(BF).astype(F32)
        a = jnp.exp2(mo - mn)
        p = jnp.where(seen, jnp.exp2(s - mn), 0.0).astype(BF)
        pv = jnp.dot(p, jnp.concatenate([nv, jnp.ones_like(nv)], axis=1), preferred_element_type=F32)
        n_s[at] = n_s[at] * a + pv[:, :hd]
        l_s[at] = l_s[at] * a + pv[:, hd:]
        m_s[at] = mn

    for b in range(nb * n_roll):
        at = (b // nb, slice(b % nb * brow, (b % nb + 1) * brow))
        o_ref[b, :brow, :] = n_s[at].astype(BF)
        total = l_s[at]
        head = total.astype(BF).astype(F32)
        aux = jnp.where(lane == 0, m_s[at], jnp.where(lane == 1, head, total - head))
        o_ref[b, brow:, :] = aux.T[:AUX].astype(BF)


def attend(hop, cl, tl, q, k, v, nk, nv, after=(), span=None, sub=512, tk=1024):
    _, brow, hd = q.shape
    roll, slots = k.shape[0], k.shape[1]
    span = span or (0, roll)
    nb = XL * NZ // roll
    rows = nb * brow
    n = span[1] - span[0]
    return pl.pallas_call(
        functools.partial(attend_kernel, hop, sub, tk, span, len(after)),
        in_specs=[ANY, ANY, VM] + [VM] * 4 + [ANY] * len(after),
        out_specs=[VM, VM],
        out_shape=[
            jax.ShapeDtypeStruct((nb * n, brow + AUX, hd), BF),
            jax.ShapeDtypeStruct((8, 128), F32),
        ],
        scratch_shapes=[pltpu.SMEM((roll,), jnp.int32)] * 2
        + [pltpu.VMEM((n, rows, hd), F32)] * 3
        + [pltpu.SemaphoreType.DMA((2,))],
        compiler_params=pltpu.CompilerParams(vmem_limit_bytes=ATTEND_VMEM),
        cost_estimate=pl.CostEstimate(
            flops=8 * n * rows * slots * hd,
            bytes_accessed=4 * n * slots * hd,
            transcendentals=n * rows * slots,
        ),
        name="attend",
    )(cl, tl, q, k, v, nk, nv, *after)


def weights_of(auxs):
    tops = [a[0:1] for a in auxs]
    sums = [a[1:2] + a[2:3] for a in auxs]
    top = functools.reduce(jnp.maximum, tops)
    ws = [jnp.exp2(t - top) for t in tops]
    total = functools.reduce(jnp.add, [w * s for w, s in zip(ws, sums)])
    return top, ws, total


def columns(rows_list):
    n = len(rows_list)
    lanes = rows_list[0].shape[1]
    pad = jnp.zeros((lanes - n, lanes), F32)
    return jnp.concatenate(list(rows_list) + [pad], axis=0).T


def merge_kernel(a_ref, b_ref, c_ref, lo_ref, hi_ref, w_ref, o_ref, first_ref, second_ref):
    half = first_ref.shape[0]
    first_ref[...] = w_ref[:half]
    second_ref[...] = w_ref[half:]
    nb, prow, lanes = o_ref.shape
    brow = prow - AUX
    cut = lo_ref.shape[0]
    for b in range(nb):
        far = (lo_ref, b) if b < cut else (hi_ref, b - cut)
        parts = ((a_ref, b), (b_ref, b), (c_ref, b), far)
        top, ws, total = weights_of([p[i, brow:, :].astype(F32) for p, i in parts])
        cols = columns(ws)
        acc = 0.0
        for n, (p, i) in enumerate(parts):
            acc = acc + cols[:, n : n + 1] * p[i, :brow, :].astype(F32)
        o_ref[b, :brow, :] = acc.astype(BF)
        head = total.astype(BF).astype(F32)
        aux = jnp.concatenate([top, head, total - head, jnp.zeros((AUX - 3, lanes), F32)], axis=0)
        o_ref[b, brow:, :] = aux.astype(BF)


def merge(parts, w):
    half = jax.ShapeDtypeStruct((w.shape[0] // 2, w.shape[1]), w.dtype)
    return pl.pallas_call(
        merge_kernel,
        in_specs=[VM] * (len(parts) + 1),
        out_specs=(VM, VM, VM),
        out_shape=(jax.ShapeDtypeStruct(parts[0].shape, BF), half, half),
        compiler_params=pltpu.CompilerParams(vmem_limit_bytes=SMALL_VMEM),
        name="merge",
    )(*parts, w)


def finish_kernel(tok, x_ref, *rest):
    o_ref = rest[-1]
    n, prow, _ = x_ref.shape
    brow = prow - AUX
    _, ws, total = weights_of([x_ref[i, brow:, :].astype(F32) for i in range(n)])
    inv = 1.0 / total
    cols = columns([w * inv for w in ws])
    acc = 0.0
    for i in range(n):
        acc = acc + cols[:, i : i + 1] * x_ref[i, :brow, :].astype(F32)
    rows = jnp.concatenate([acc[g * tok : (g + 1) * tok] for g in range(brow // tok)], axis=1)
    pair = jnp.concatenate([rows, rows], axis=0).astype(BF)
    step = 2 * tok
    for c in range(n // 2):
        o_ref[c * step : (c + 1) * step, :] = pair


def finish(x, tok, after):
    n, prow, hd = x.shape
    width = (prow - AUX) // tok * hd
    return pl.pallas_call(
        functools.partial(finish_kernel, tok),
        in_specs=[VM] + [ANY] * len(after),
        out_specs=VM,
        out_shape=jax.ShapeDtypeStruct((n * tok, width), BF),
        compiler_params=pltpu.CompilerParams(vmem_limit_bytes=SMALL_VMEM),
        name="finish",
    )(x, *after)


def project_kernel(a_ref, w_ref, *rest):
    o_ref = rest[-1]
    half = w_ref.shape[0] // 2
    y = lax.axis_index("y")
    pieces = [(w_ref.at[:half], w_ref.at[half:])] + [rest[2 * i : 2 * i + 2] for i in range(NY - 1)]
    for k, (top, low) in enumerate(pieces):
        out = jnp.dot(a_ref[:, :half], top[...], preferred_element_type=F32)
        out = out + jnp.dot(a_ref[:, half:], low[...], preferred_element_type=F32)
        o_ref[lax.rem(y - k + NY, NY)] = out.astype(BF)


def project(a, w, others):
    return pl.pallas_call(
        project_kernel,
        in_specs=[VM] * (2 + len(others)),
        out_specs=VM,
        out_shape=jax.ShapeDtypeStruct((NY, a.shape[0], w.shape[1]), BF),
        compiler_params=pltpu.CompilerParams(vmem_limit_bytes=SMALL_VMEM),
        name="project",
    )(a, w, *others)


def shift(x, k):
    return lax.ppermute(x, "y", [(i, (i + k) % NY) for i in range(NY)])


def on_device(queries, new_keys, new_values, cache_keys, cache_values, out_weight, context_lengths, turn_lengths):
    tok, q_width = queries.shape
    hd = cache_keys.shape[3]
    groups = q_width // hd
    roll = cache_keys.shape[1]
    blocks = XL * NZ
    brow = groups * tok
    plane = ("xl", "z")

    rows = queries.reshape(tok, groups, hd).transpose(1, 0, 2).reshape(1, brow, hd)
    half = q_width // 2
    up1, low3 = shift(out_weight[:half], 1), shift(out_weight[half:], 3)
    q0 = lax.all_to_all(jnp.broadcast_to(rows, (blocks, brow, hd)), plane, 0, 0, tiled=True)
    near = {k: shift(q0, k) for k in (1, 3)}
    cut = blocks // 2
    far = (shift(near[1][:cut], 1), shift(near[3][cut:], 3))
    lens = (context_lengths, turn_lengths)
    kv = prepare(cache_keys[0], cache_values[0], new_keys, new_values)

    own, token = attend(0, *lens, q0, *kv, after=(up1, low3))

    def away(k, q, span=None, after=()):
        return shift(attend(k, *lens, q, *kv, after=(token,) + after, span=span)[0], -k)

    hi = away(2, far[1], (roll // 2, roll))
    one, three = away(1, near[1]), away(3, near[3], after=far)
    lo = away(2, far[0], (0, roll // 2))
    merged, top, low = merge([own, one, three, lo, hi], out_weight)

    up3, low1 = shift(top, 3), shift(low, 1)
    gathered = lax.all_to_all(merged, plane, 0, 0, tiled=True)
    copies = finish(gathered, tok, (up3, low1))
    up2, low2 = shift(up1, 1), shift(low3, 3)
    attended = lax.all_to_all(copies, plane, 0, 0, tiled=True).reshape(blocks * tok, q_width)
    width = out_weight.shape[1]
    rb = blocks * tok // roll
    mine = project(attended, out_weight, (up1, low1, up2, low2, up3, low3))
    got = lax.all_to_all(mine.reshape(NY * roll, rb, width), ("y",) + HEAD, 0, 0, tiled=True)
    total = jnp.sum(got.reshape(NY, roll, rb // tok, tok, width).astype(F32), axis=1)
    return total.astype(BF).transpose(1, 0, 2, 3).reshape(NY * rb, width)


def solution(mesh):
    fine = Mesh(mesh.devices.reshape(XL, NZ, NY, XH, CORE), ("xl", "z", "y", "xh", "core"))
    in_specs = (
        P(CTX, HEAD),
        P(CTX, HEAD),
        P(CTX, HEAD),
        P(HEAD, None, CTX, None),
        P(HEAD, None, CTX, None),
        P(HEAD, CTX),
        P(),
        P(),
    )
    return jax.shard_map(
        on_device, mesh=fine, in_specs=in_specs, out_specs=P(HEAD, CTX), check_vma=False
    )
```

```python
import functools

import jax
import jax.numpy as jnp
from jax import lax
from jax.experimental import pallas as pl
from jax.experimental.pallas import tpu as pltpu
from jax.sharding import Mesh
from jax.sharding import PartitionSpec as P

FLOOR = -(2.0**99)
LOG2E = 1.4426950408889634
BF = jnp.bfloat16
F32 = jnp.float32
AUX = 16
XL, NZ, NY, XH, CORE = 2, 8, 4, 2, 2
VM = pl.BlockSpec(memory_space=pltpu.VMEM)
ANY = pl.BlockSpec(memory_space=pl.ANY)
CTX = ("xl", "z", "y")
HEAD = ("xh", "core")
ATTEND_VMEM = 36 * 2**20
SMALL_VMEM = 16 * 2**20


def dot_t(a, b):
    return lax.dot_general(a, b, (((1,), (1,)), ((), ())), preferred_element_type=F32)


def prepare_kernel(k_in, v_in, nk_in, nv_in, k_out, v_out, nk_out, nv_out, sems):
    pairs = ((k_in, k_out), (v_in, v_out), (nk_in, nk_out), (nv_in, nv_out))
    copies = [pltpu.make_async_copy(a, b, sems.at[i]) for i, (a, b) in enumerate(pairs)]
    for c in copies:
        c.start()
    for c in copies:
        c.wait()


def prepare(*given):
    return pl.pallas_call(
        prepare_kernel,
        in_specs=[ANY] * len(given),
        out_specs=[VM] * len(given),
        out_shape=[jax.ShapeDtypeStruct(a.shape, a.dtype) for a in given],
        scratch_shapes=[pltpu.SemaphoreType.DMA((len(given),))],
        compiler_params=pltpu.CompilerParams(vmem_limit_bytes=SMALL_VMEM),
        name="prepare",
    )(*given)


def attend_kernel(hop, sub, span, n_after, cl_hbm, tl_hbm, q_ref, k_ref, v_ref, nk_ref, nv_ref, *rest):
    o_ref, token, cl_ref, tl_ref, n_s, l_s, m_s, sems = rest[n_after : n_after + 8]
    token[...] = jnp.zeros_like(token)
    blocks, brow, hd = q_ref.shape
    roll, slots = k_ref.shape[0], k_ref.shape[1]
    nb = XL * NZ // roll
    nblk = nb * roll
    held = 0 if blocks == nblk else span[0]
    rows = nb * brow
    tok = nk_ref.shape[0]
    small = [
        pltpu.make_async_copy(cl_hbm, cl_ref, sems.at[0]),
        pltpu.make_async_copy(tl_hbm, tl_ref, sems.at[1]),
    ]
    for c in small:
        c.start()
    for c in small:
        c.wait()
    y = lax.axis_index("y")
    ctx = (lax.axis_index("xl") * NZ + lax.axis_index("z")) * NY + y
    per_roll = nblk * NY // roll
    own = lax.div(ctx, per_roll)
    first = lax.rem(ctx, per_roll) * tok
    off = lax.rem(y - hop + NY, NY) * tok
    lane = lax.broadcasted_iota(jnp.int32, (brow, hd), 1)

    n_roll = span[1] - span[0]
    slot_of = lax.broadcasted_iota(jnp.int32, (1, slots), 1)
    per = sub // brow
    each = rows // sub

    def split(base, count):
        qf = q_ref[pl.ds(base, count)].reshape(count * brow, hd).astype(F32) * (hd**-0.5 * LOG2E)
        hi = qf.astype(BF)
        lo = (qf - hi.astype(F32)).astype(BF)
        return jnp.concatenate([hi, lo], axis=1)

    def seen_slots(r):
        return jnp.clip(cl_ref[r] - ctx * slots, 0, slots)

    def score(r, i):
        k = k_ref[r]
        s = dot_t(split((r - held) * nb + i * per, per), jnp.concatenate([k, k], axis=1))
        return jnp.where(slot_of < seen_slots(r), s, FLOOR)

    def together(p, carry):
        steps = [(span[0] + 2 * p + x, i) for x in range(2) for i in range(each)]
        ahead = score(*steps[0])
        for x, (r, i) in enumerate(steps):
            s = ahead
            if x + 1 < len(steps):
                ahead = score(*steps[x + 1])
            m = jnp.max(s, axis=1, keepdims=True).astype(BF).astype(F32)
            p_ = jnp.exp2(s - m).astype(BF)
            v = v_ref[r]
            pv = jnp.dot(p_, jnp.concatenate([v, jnp.ones_like(v)], axis=1), preferred_element_type=F32)
            at = (r - span[0], slice(i * sub, (i + 1) * sub))
            some = seen_slots(r) > 0
            n_s[at] = jnp.where(some, pv[:, :hd], 0.0)
            l_s[at] = jnp.where(some, pv[:, hd:], 0.0)
            m_s[at] = jnp.broadcast_to(m, (sub, hd))
        return carry

    lax.fori_loop(0, n_roll // 2, together, 0)

    @pl.when((own >= span[0]) & (own < span[1]))
    def _():
        pad = jnp.zeros((hd - tok, hd), F32)
        nk = jnp.concatenate([nk_ref[...].astype(F32), pad], axis=0).astype(BF)
        nv = jnp.concatenate([nv_ref[...].astype(F32), pad], axis=0).astype(BF)
        s = dot_t(split((own - held) * nb, nb), jnp.concatenate([nk, nk], axis=1))
        row = lax.broadcasted_iota(jnp.int32, s.shape, 0)
        col = lax.broadcasted_iota(jnp.int32, s.shape, 1)
        t = (row // brow) * (NY * tok) + off + row % tok
        j = first + col
        seen = (col < tok) & (j <= t) & (j < tl_ref[own])
        s = jnp.where(seen, s, FLOOR)
        at = own - span[0]
        mo = m_s[at]
        mn = jnp.maximum(mo, jnp.max(s, axis=1, keepdims=True)).astype(BF).astype(F32)
        a = jnp.exp2(mo - mn)
        p = jnp.where(seen, jnp.exp2(s - mn), 0.0).astype(BF)
        pv = jnp.dot(p, jnp.concatenate([nv, jnp.ones_like(nv)], axis=1), preferred_element_type=F32)
        n_s[at] = n_s[at] * a + pv[:, :hd]
        l_s[at] = l_s[at] * a + pv[:, hd:]
        m_s[at] = mn

    def emit(x, carry):
        for b in range(nb):
            at = (x, slice(b * brow, (b + 1) * brow))
            out = x * nb + b
            o_ref[out, :brow, :] = n_s[at].astype(BF)
            total = l_s[at]
            head = total.astype(BF).astype(F32)
            aux = jnp.where(lane == 0, m_s[at], jnp.where(lane == 1, head, total - head))
            o_ref[out, brow:, :] = aux.T[:AUX].astype(BF)
        return carry

    lax.fori_loop(0, n_roll, emit, 0)


def attend(hop, cl, tl, q, k, v, nk, nv, after=(), span=None, sub=256):
    _, brow, hd = q.shape
    roll, slots = k.shape[0], k.shape[1]
    span = span or (0, roll)
    nb = XL * NZ // roll
    rows = nb * brow
    n = span[1] - span[0]
    return pl.pallas_call(
        functools.partial(attend_kernel, hop, sub, span, len(after)),
        in_specs=[ANY, ANY, VM] + [VM] * 4 + [ANY] * len(after),
        out_specs=[VM, VM],
        out_shape=[
            jax.ShapeDtypeStruct((nb * n, brow + AUX, hd), BF),
            jax.ShapeDtypeStruct((8, 128), F32),
        ],
        scratch_shapes=[pltpu.SMEM((roll,), jnp.int32)] * 2
        + [pltpu.VMEM((n, rows, hd), F32)] * 3
        + [pltpu.SemaphoreType.DMA((2,))],
        compiler_params=pltpu.CompilerParams(vmem_limit_bytes=ATTEND_VMEM),
        cost_estimate=pl.CostEstimate(
            flops=8 * n * rows * slots * hd,
            bytes_accessed=4 * n * slots * hd,
            transcendentals=n * rows * slots,
        ),
        name="attend",
    )(cl, tl, q, k, v, nk, nv, *after)


def weights_of(auxs):
    tops = [a[0:1] for a in auxs]
    sums = [a[1:2] + a[2:3] for a in auxs]
    top = functools.reduce(jnp.maximum, tops)
    ws = [jnp.exp2(t - top) for t in tops]
    total = functools.reduce(jnp.add, [w * s for w, s in zip(ws, sums)])
    return top, ws, total


def columns(rows_list):
    n = len(rows_list)
    lanes = rows_list[0].shape[1]
    pad = jnp.zeros((lanes - n, lanes), F32)
    return jnp.concatenate(list(rows_list) + [pad], axis=0).T


def merge_kernel(a_ref, b_ref, c_ref, lo_ref, hi_ref, w_ref, o_ref, first_ref, second_ref):
    half = first_ref.shape[0]
    first_ref[...] = w_ref[:half]
    second_ref[...] = w_ref[half:]
    nb, prow, lanes = o_ref.shape
    brow = prow - AUX
    cut = lo_ref.shape[0]
    for b in range(nb):
        far = (lo_ref, b) if b < cut else (hi_ref, b - cut)
        parts = ((a_ref, b), (b_ref, b), (c_ref, b), far)
        top, ws, total = weights_of([p[i, brow:, :].astype(F32) for p, i in parts])
        cols = columns(ws)
        acc = 0.0
        for n, (p, i) in enumerate(parts):
            acc = acc + cols[:, n : n + 1] * p[i, :brow, :].astype(F32)
        o_ref[b, :brow, :] = acc.astype(BF)
        head = total.astype(BF).astype(F32)
        aux = jnp.concatenate([top, head, total - head, jnp.zeros((AUX - 3, lanes), F32)], axis=0)
        o_ref[b, brow:, :] = aux.astype(BF)


def merge(parts, w):
    half = jax.ShapeDtypeStruct((w.shape[0] // 2, w.shape[1]), w.dtype)
    return pl.pallas_call(
        merge_kernel,
        in_specs=[VM] * (len(parts) + 1),
        out_specs=(VM, VM, VM),
        out_shape=(jax.ShapeDtypeStruct(parts[0].shape, BF), half, half),
        compiler_params=pltpu.CompilerParams(vmem_limit_bytes=SMALL_VMEM),
        name="merge",
    )(*parts, w)


def finish_kernel(tok, x_ref, *rest):
    o_ref = rest[-1]
    n, prow, _ = x_ref.shape
    brow = prow - AUX
    _, ws, total = weights_of([x_ref[i, brow:, :].astype(F32) for i in range(n)])
    inv = 1.0 / total
    cols = columns([w * inv for w in ws])
    acc = 0.0
    for i in range(n):
        acc = acc + cols[:, i : i + 1] * x_ref[i, :brow, :].astype(F32)
    rows = jnp.concatenate([acc[g * tok : (g + 1) * tok] for g in range(brow // tok)], axis=1)
    pair = jnp.concatenate([rows, rows], axis=0).astype(BF)
    step = 2 * tok
    for c in range(n // 2):
        o_ref[c * step : (c + 1) * step, :] = pair


def finish(x, tok, after):
    n, prow, hd = x.shape
    width = (prow - AUX) // tok * hd
    return pl.pallas_call(
        functools.partial(finish_kernel, tok),
        in_specs=[VM] + [ANY] * len(after),
        out_specs=VM,
        out_shape=jax.ShapeDtypeStruct((n * tok, width), BF),
        compiler_params=pltpu.CompilerParams(vmem_limit_bytes=SMALL_VMEM),
        name="finish",
    )(x, *after)


def project_kernel(a_ref, w_ref, *rest):
    o_ref = rest[-1]
    half = w_ref.shape[0] // 2
    y = lax.axis_index("y")
    pieces = [(w_ref.at[:half], w_ref.at[half:])] + [rest[2 * i : 2 * i + 2] for i in range(NY - 1)]
    for k, (top, low) in enumerate(pieces):
        out = jnp.dot(a_ref[:, :half], top[...], preferred_element_type=F32)
        out = out + jnp.dot(a_ref[:, half:], low[...], preferred_element_type=F32)
        o_ref[lax.rem(y - k + NY, NY)] = out.astype(BF)


def project(a, w, others):
    return pl.pallas_call(
        project_kernel,
        in_specs=[VM] * (2 + len(others)),
        out_specs=VM,
        out_shape=jax.ShapeDtypeStruct((NY, a.shape[0], w.shape[1]), BF),
        compiler_params=pltpu.CompilerParams(vmem_limit_bytes=SMALL_VMEM),
        name="project",
    )(a, w, *others)


def shift(x, k):
    return lax.ppermute(x, "y", [(i, (i + k) % NY) for i in range(NY)])


def on_device(queries, new_keys, new_values, cache_keys, cache_values, out_weight, context_lengths, turn_lengths):
    tok, q_width = queries.shape
    hd = cache_keys.shape[3]
    groups = q_width // hd
    roll = cache_keys.shape[1]
    blocks = XL * NZ
    brow = groups * tok
    plane = ("xl", "z")

    rows = queries.reshape(tok, groups, hd).transpose(1, 0, 2).reshape(1, brow, hd)
    half = q_width // 2
    up1, low3 = shift(out_weight[:half], 1), shift(out_weight[half:], 3)
    q0 = lax.all_to_all(jnp.broadcast_to(rows, (blocks, brow, hd)), plane, 0, 0, tiled=True)
    near = {k: shift(q0, k) for k in (1, 3)}
    cut = blocks // 2
    far = (shift(near[1][:cut], 1), shift(near[3][cut:], 3))
    lens = (context_lengths, turn_lengths)
    kv = prepare(cache_keys[0], cache_values[0], new_keys, new_values)

    own, token = attend(0, *lens, q0, *kv, after=(up1, low3))

    def away(k, q, span=None, after=()):
        return shift(attend(k, *lens, q, *kv, after=(token,) + after, span=span)[0], -k)

    hi = away(2, far[1], (roll // 2, roll))
    one, three = away(1, near[1]), away(3, near[3], after=far)
    lo = away(2, far[0], (0, roll // 2))
    merged, top, low = merge([own, one, three, lo, hi], out_weight)

    up3, low1 = shift(top, 3), shift(low, 1)
    gathered = lax.all_to_all(merged, plane, 0, 0, tiled=True)
    copies = finish(gathered, tok, (up3, low1))
    up2, low2 = shift(up1, 1), shift(low3, 3)
    attended = lax.all_to_all(copies, plane, 0, 0, tiled=True).reshape(blocks * tok, q_width)
    width = out_weight.shape[1]
    rb = blocks * tok // roll
    mine = project(attended, out_weight, (up1, low1, up2, low2, up3, low3))
    got = lax.all_to_all(mine.reshape(NY * roll, rb, width), ("y",) + HEAD, 0, 0, tiled=True)
    total = jnp.sum(got.reshape(NY, roll, rb // tok, tok, width).astype(F32), axis=1)
    return total.astype(BF).transpose(1, 0, 2, 3).reshape(NY * rb, width)


def solution(mesh):
    fine = Mesh(mesh.devices.reshape(XL, NZ, NY, XH, CORE), ("xl", "z", "y", "xh", "core"))
    in_specs = (
        P(CTX, HEAD),
        P(CTX, HEAD),
        P(CTX, HEAD),
        P(HEAD, None, CTX, None),
        P(HEAD, None, CTX, None),
        P(HEAD, CTX),
        P(),
        P(),
    )
    return jax.shard_map(
        on_device, mesh=fine, in_specs=in_specs, out_specs=P(HEAD, CTX), check_vma=False
    )
```

```python
import functools

import jax
import jax.numpy as jnp
from jax import lax
from jax.experimental import pallas as pl
from jax.experimental.pallas import tpu as pltpu
from jax.sharding import Mesh
from jax.sharding import PartitionSpec as P

FLOOR = -(2.0**99)
LOG2E = 1.4426950408889634
BF = jnp.bfloat16
F32 = jnp.float32
AUX = 16
XL, NZ, NY, XH, CORE = 2, 8, 4, 2, 2
VM = pl.BlockSpec(memory_space=pltpu.VMEM)
ANY = pl.BlockSpec(memory_space=pl.ANY)
CTX = ("xl", "z", "y")
HEAD = ("xh", "core")
ATTEND_VMEM = 36 * 2**20
SMALL_VMEM = 16 * 2**20


def dot_t(a, b):
    return lax.dot_general(a, b, (((1,), (1,)), ((), ())), preferred_element_type=F32)


def prepare_kernel(k_in, v_in, nk_in, nv_in, k_out, v_out, nk_out, nv_out, sems):
    pairs = ((k_in, k_out), (v_in, v_out), (nk_in, nk_out), (nv_in, nv_out))
    copies = [pltpu.make_async_copy(a, b, sems.at[i]) for i, (a, b) in enumerate(pairs)]
    for c in copies:
        c.start()
    for c in copies:
        c.wait()


def prepare(*given):
    return pl.pallas_call(
        prepare_kernel,
        in_specs=[ANY] * len(given),
        out_specs=[VM] * len(given),
        out_shape=[jax.ShapeDtypeStruct(a.shape, a.dtype) for a in given],
        scratch_shapes=[pltpu.SemaphoreType.DMA((len(given),))],
        compiler_params=pltpu.CompilerParams(vmem_limit_bytes=SMALL_VMEM),
        name="prepare",
    )(*given)


def attend_kernel(hops, sub, span, n_after, cl_hbm, tl_hbm, k_ref, v_ref, nk_ref, nv_ref, *rest):
    two = len(hops)
    q_refs, outs = rest[:two], rest[two + n_after : two + n_after + two]
    token, cl_ref, tl_ref, n_s, l_s, m_s, sems = rest[two + n_after + two : two + n_after + two + 7]
    q_ref = q_refs[0]
    if two == 2:
        q_ref = rest[-1]
        mid = q_ref.shape[0] // 2
        q_ref[:mid] = q_refs[0][:mid]
        q_ref[mid:] = q_refs[1][mid:]
    token[...] = jnp.zeros_like(token)
    blocks, brow, hd = q_ref.shape
    roll, slots = k_ref.shape[0], k_ref.shape[1]
    nb = XL * NZ // roll
    nblk = nb * roll
    held = 0 if blocks == nblk else span[0]
    rows = nb * brow
    tok = nk_ref.shape[0]
    small = [
        pltpu.make_async_copy(cl_hbm, cl_ref, sems.at[0]),
        pltpu.make_async_copy(tl_hbm, tl_ref, sems.at[1]),
    ]
    for c in small:
        c.start()
    for c in small:
        c.wait()
    y = lax.axis_index("y")
    ctx = (lax.axis_index("xl") * NZ + lax.axis_index("z")) * NY + y
    per_roll = nblk * NY // roll
    own = lax.div(ctx, per_roll)
    first = lax.rem(ctx, per_roll) * tok
    hop = hops[0] if two == 1 else jnp.where(own < roll // 2, hops[0], hops[1])
    off = lax.rem(y - hop + NY, NY) * tok
    lane = lax.broadcasted_iota(jnp.int32, (brow, hd), 1)

    n_roll = span[1] - span[0]
    slot_of = lax.broadcasted_iota(jnp.int32, (1, slots), 1)
    per = sub // brow
    each = rows // sub

    def split(base, count):
        qf = q_ref[pl.ds(base, count)].reshape(count * brow, hd).astype(F32) * (hd**-0.5 * LOG2E)
        hi = qf.astype(BF)
        lo = (qf - hi.astype(F32)).astype(BF)
        return jnp.concatenate([hi, lo], axis=1)

    def seen_slots(r):
        return jnp.clip(cl_ref[r] - ctx * slots, 0, slots)

    def score(r, i):
        k = k_ref[r]
        s = dot_t(split((r - held) * nb + i * per, per), jnp.concatenate([k, k], axis=1))
        return jnp.where(slot_of < seen_slots(r), s, FLOOR)

    def together(p, carry):
        steps = [(span[0] + 2 * p + x, i) for x in range(2) for i in range(each)]
        ahead = score(*steps[0])
        for x, (r, i) in enumerate(steps):
            s = ahead
            if x + 1 < len(steps):
                ahead = score(*steps[x + 1])
            m = jnp.max(s, axis=1, keepdims=True).astype(BF).astype(F32)
            p_ = jnp.exp2(s - m).astype(BF)
            v = v_ref[r]
            pv = jnp.dot(p_, jnp.concatenate([v, jnp.ones_like(v)], axis=1), preferred_element_type=F32)
            at = (r - span[0], slice(i * sub, (i + 1) * sub))
            some = seen_slots(r) > 0
            n_s[at] = jnp.where(some, pv[:, :hd], 0.0)
            l_s[at] = jnp.where(some, pv[:, hd:], 0.0)
            m_s[at] = jnp.broadcast_to(m, (sub, hd))
        return carry

    lax.fori_loop(0, n_roll // 2, together, 0)

    @pl.when((own >= span[0]) & (own < span[1]))
    def _():
        pad = jnp.zeros((hd - tok, hd), F32)
        nk = jnp.concatenate([nk_ref[...].astype(F32), pad], axis=0).astype(BF)
        nv = jnp.concatenate([nv_ref[...].astype(F32), pad], axis=0).astype(BF)
        s = dot_t(split((own - held) * nb, nb), jnp.concatenate([nk, nk], axis=1))
        row = lax.broadcasted_iota(jnp.int32, s.shape, 0)
        col = lax.broadcasted_iota(jnp.int32, s.shape, 1)
        t = (row // brow) * (NY * tok) + off + row % tok
        j = first + col
        seen = (col < tok) & (j <= t) & (j < tl_ref[own])
        s = jnp.where(seen, s, FLOOR)
        at = own - span[0]
        mo = m_s[at]
        mn = jnp.maximum(mo, jnp.max(s, axis=1, keepdims=True)).astype(BF).astype(F32)
        a = jnp.exp2(mo - mn)
        p = jnp.where(seen, jnp.exp2(s - mn), 0.0).astype(BF)
        pv = jnp.dot(p, jnp.concatenate([nv, jnp.ones_like(nv)], axis=1), preferred_element_type=F32)
        n_s[at] = n_s[at] * a + pv[:, :hd]
        l_s[at] = l_s[at] * a + pv[:, hd:]
        m_s[at] = mn

    for half, o_ref in enumerate(outs):

        def emit(x, carry):
            for b in range(nb):
                at = (x + half * (n_roll // two), slice(b * brow, (b + 1) * brow))
                out = x * nb + b
                o_ref[out, :brow, :] = n_s[at].astype(BF)
                total = l_s[at]
                head = total.astype(BF).astype(F32)
                aux = jnp.where(lane == 0, m_s[at], jnp.where(lane == 1, head, total - head))
                o_ref[out, brow:, :] = aux.T[:AUX].astype(BF)
            return carry

        lax.fori_loop(0, n_roll // two, emit, 0)


def attend(hops, cl, tl, qs, k, v, nk, nv, after=(), span=None, sub=256):
    brow, hd = qs[0].shape[1:]
    roll, slots = k.shape[0], k.shape[1]
    span = span or (0, roll)
    nb = XL * NZ // roll
    rows = nb * brow
    n = span[1] - span[0]
    two = len(hops)
    part = jax.ShapeDtypeStruct((nb * n // two, brow + AUX, hd), BF)
    return pl.pallas_call(
        functools.partial(attend_kernel, hops, sub, span, len(after)),
        in_specs=[ANY, ANY] + [VM] * (4 + two) + [ANY] * len(after),
        out_specs=[VM] * (two + 1),
        out_shape=[part] * two + [jax.ShapeDtypeStruct((8, 128), F32)],
        scratch_shapes=[pltpu.SMEM((roll,), jnp.int32)] * 2
        + [pltpu.VMEM((n, rows, hd), F32)] * 3
        + [pltpu.SemaphoreType.DMA((2,))]
        + ([pltpu.VMEM(qs[0].shape, BF)] if two == 2 else []),
        compiler_params=pltpu.CompilerParams(vmem_limit_bytes=ATTEND_VMEM),
        cost_estimate=pl.CostEstimate(
            flops=8 * n * rows * slots * hd,
            bytes_accessed=4 * n * slots * hd,
            transcendentals=n * rows * slots,
        ),
        name="attend",
    )(cl, tl, k, v, nk, nv, *qs, *after)


def weights_of(auxs):
    tops = [a[0:1] for a in auxs]
    sums = [a[1:2] + a[2:3] for a in auxs]
    top = functools.reduce(jnp.maximum, tops)
    ws = [jnp.exp2(t - top) for t in tops]
    total = functools.reduce(jnp.add, [w * s for w, s in zip(ws, sums)])
    return top, ws, total


def columns(rows_list):
    n = len(rows_list)
    lanes = rows_list[0].shape[1]
    pad = jnp.zeros((lanes - n, lanes), F32)
    return jnp.concatenate(list(rows_list) + [pad], axis=0).T


def merge_kernel(passed, *refs):
    n_in = len(refs) - 1 - 2 * passed if passed else len(refs) - 1
    whole, halves = refs[0], refs[1 : n_in - passed]
    o_ref = refs[n_in]
    if passed:
        w_ref, first_ref, second_ref = refs[n_in - 1], refs[n_in + 1], refs[n_in + 2]
        half = first_ref.shape[0]
        first_ref[...] = w_ref[:half]
        second_ref[...] = w_ref[half:]
    nb, prow, lanes = o_ref.shape
    brow = prow - AUX
    cut = nb // 2
    for b in range(nb):
        side = b // cut
        parts = [(whole, b)] + [(p, b - side * cut) for p in halves[side::2]]
        top, ws, total = weights_of([p[i, brow:, :].astype(F32) for p, i in parts])
        cols = columns(ws)
        acc = 0.0
        for n, (p, i) in enumerate(parts):
            acc = acc + cols[:, n : n + 1] * p[i, :brow, :].astype(F32)
        o_ref[b, :brow, :] = acc.astype(BF)
        head = total.astype(BF).astype(F32)
        aux = jnp.concatenate([top, head, total - head, jnp.zeros((AUX - 3, lanes), F32)], axis=0)
        o_ref[b, brow:, :] = aux.astype(BF)


def merge(parts, w=None):
    out = [jax.ShapeDtypeStruct(parts[0].shape, BF)]
    given = list(parts)
    if w is not None:
        given.append(w)
        out += [jax.ShapeDtypeStruct((w.shape[0] // 2, w.shape[1]), w.dtype)] * 2
    return pl.pallas_call(
        functools.partial(merge_kernel, int(w is not None)),
        in_specs=[VM] * len(given),
        out_specs=[VM] * len(out),
        out_shape=out,
        compiler_params=pltpu.CompilerParams(vmem_limit_bytes=SMALL_VMEM),
        name="merge",
    )(*given)


def finish_kernel(tok, x_ref, *rest):
    o_ref = rest[-1]
    n, prow, _ = x_ref.shape
    brow = prow - AUX
    _, ws, total = weights_of([x_ref[i, brow:, :].astype(F32) for i in range(n)])
    inv = 1.0 / total
    cols = columns([w * inv for w in ws])
    acc = 0.0
    for i in range(n):
        acc = acc + cols[:, i : i + 1] * x_ref[i, :brow, :].astype(F32)
    rows = jnp.concatenate([acc[g * tok : (g + 1) * tok] for g in range(brow // tok)], axis=1)
    pair = jnp.concatenate([rows, rows], axis=0).astype(BF)
    step = 2 * tok
    for c in range(n // 2):
        o_ref[c * step : (c + 1) * step, :] = pair


def finish(x, tok, after):
    n, prow, hd = x.shape
    width = (prow - AUX) // tok * hd
    return pl.pallas_call(
        functools.partial(finish_kernel, tok),
        in_specs=[VM] + [ANY] * len(after),
        out_specs=VM,
        out_shape=jax.ShapeDtypeStruct((n * tok, width), BF),
        compiler_params=pltpu.CompilerParams(vmem_limit_bytes=SMALL_VMEM),
        name="finish",
    )(x, *after)


def project_kernel(a_ref, w_ref, *rest):
    o_ref = rest[-1]
    half = w_ref.shape[0] // 2
    y = lax.axis_index("y")
    pieces = [(w_ref.at[:half], w_ref.at[half:])] + [rest[2 * i : 2 * i + 2] for i in range(NY - 1)]
    for k, (top, low) in enumerate(pieces):
        out = jnp.dot(a_ref[:, :half], top[...], preferred_element_type=F32)
        out = out + jnp.dot(a_ref[:, half:], low[...], preferred_element_type=F32)
        o_ref[lax.rem(y - k + NY, NY)] = out.astype(BF)


def project(a, w, others):
    return pl.pallas_call(
        project_kernel,
        in_specs=[VM] * (2 + len(others)),
        out_specs=VM,
        out_shape=jax.ShapeDtypeStruct((NY, a.shape[0], w.shape[1]), BF),
        compiler_params=pltpu.CompilerParams(vmem_limit_bytes=SMALL_VMEM),
        name="project",
    )(a, w, *others)


def shift(x, k):
    return lax.ppermute(x, "y", [(i, (i + k) % NY) for i in range(NY)])


def on_device(queries, new_keys, new_values, cache_keys, cache_values, out_weight, context_lengths, turn_lengths):
    tok, q_width = queries.shape
    hd = cache_keys.shape[3]
    groups = q_width // hd
    roll = cache_keys.shape[1]
    blocks = XL * NZ
    brow = groups * tok
    plane = ("xl", "z")

    rows = queries.reshape(tok, groups, hd).transpose(1, 0, 2).reshape(1, brow, hd)
    half = q_width // 2
    up1, low3 = shift(out_weight[:half], 1), shift(out_weight[half:], 3)
    q0 = lax.all_to_all(jnp.broadcast_to(rows, (blocks, brow, hd)), plane, 0, 0, tiled=True)
    near = {k: shift(q0, k) for k in (1, 3)}
    cut = blocks // 2
    far = (shift(near[1][:cut], 1), shift(near[3][cut:], 3))
    lens = (context_lengths, turn_lengths)
    kv = prepare(cache_keys[0], cache_values[0], new_keys, new_values)

    own, token = attend((0,), *lens, (q0,), *kv, after=(up1, low3))

    def away(hops, qs, span=None, after=()):
        *parts, _ = attend(hops, *lens, qs, *kv, after=(token,) + after, span=span)
        return [shift(p, -k) for p, k in zip(parts, hops)]

    (hi2,) = away((2,), far[1:], (roll // 2, roll))
    lo1, hi3 = away((1, 3), (near[1], near[3]))
    lo3, hi1 = away((3, 1), (near[3], near[1]), after=far)
    (lo2,) = away((2,), far[:1], (0, roll // 2))
    (early,) = merge([own, lo1, hi1, lo3, hi3])
    merged, top, low = merge([early, lo2, hi2], out_weight)

    up3, low1 = shift(top, 3), shift(low, 1)
    gathered = lax.all_to_all(merged, plane, 0, 0, tiled=True)
    copies = finish(gathered, tok, (up3, low1))
    up2, low2 = shift(up1, 1), shift(low3, 3)
    attended = lax.all_to_all(copies, plane, 0, 0, tiled=True).reshape(blocks * tok, q_width)
    width = out_weight.shape[1]
    rb = blocks * tok // roll
    mine = project(attended, out_weight, (up1, low1, up2, low2, up3, low3))
    got = lax.all_to_all(mine.reshape(NY * roll, rb, width), ("y",) + HEAD, 0, 0, tiled=True)
    total = jnp.sum(got.reshape(NY, roll, rb // tok, tok, width).astype(F32), axis=1)
    return total.astype(BF).transpose(1, 0, 2, 3).reshape(NY * rb, width)


def solution(mesh):
    fine = Mesh(mesh.devices.reshape(XL, NZ, NY, XH, CORE), ("xl", "z", "y", "xh", "core"))
    in_specs = (
        P(CTX, HEAD),
        P(CTX, HEAD),
        P(CTX, HEAD),
        P(HEAD, None, CTX, None),
        P(HEAD, None, CTX, None),
        P(HEAD, CTX),
        P(),
        P(),
    )
    return jax.shard_map(
        on_device, mesh=fine, in_specs=in_specs, out_specs=P(HEAD, CTX), check_vma=False
    )
```

```python
import functools

import jax
import jax.numpy as jnp
from jax import lax
from jax.experimental import pallas as pl
from jax.experimental.pallas import tpu as pltpu
from jax.sharding import Mesh
from jax.sharding import PartitionSpec as P

FLOOR = -(2.0**99)
LOG2E = 1.4426950408889634
BF = jnp.bfloat16
F32 = jnp.float32
AUX = 16
XL, NZ, NY, XH, CORE = 2, 8, 4, 2, 2
VM = pl.BlockSpec(memory_space=pltpu.VMEM)
ANY = pl.BlockSpec(memory_space=pl.ANY)
CTX = ("xl", "z", "y")
HEAD = ("xh", "core")
ATTEND_VMEM = 36 * 2**20
SMALL_VMEM = 16 * 2**20


def dot_t(a, b):
    return lax.dot_general(a, b, (((1,), (1,)), ((), ())), preferred_element_type=F32)


def prepare_kernel(k_in, v_in, nk_in, nv_in, k_out, v_out, nk_out, nv_out, sems):
    pairs = ((k_in, k_out), (v_in, v_out), (nk_in, nk_out), (nv_in, nv_out))
    copies = [pltpu.make_async_copy(a, b, sems.at[i]) for i, (a, b) in enumerate(pairs)]
    for c in copies:
        c.start()
    for c in copies:
        c.wait()


def prepare(*given):
    return pl.pallas_call(
        prepare_kernel,
        in_specs=[ANY] * len(given),
        out_specs=[VM] * len(given),
        out_shape=[jax.ShapeDtypeStruct(a.shape, a.dtype) for a in given],
        scratch_shapes=[pltpu.SemaphoreType.DMA((len(given),))],
        compiler_params=pltpu.CompilerParams(vmem_limit_bytes=SMALL_VMEM),
        name="prepare",
    )(*given)


def attend_kernel(hops, sub, span, n_after, cl_hbm, tl_hbm, k_ref, v_ref, nk_ref, nv_ref, *rest):
    two = len(hops)
    q_refs, outs = rest[:two], rest[two + n_after : two + n_after + two]
    token, cl_ref, tl_ref, n_s, l_s, m_s, sems = rest[two + n_after + two : two + n_after + two + 7]
    q_ref = q_refs[0]
    if two == 2:
        q_ref = rest[-1]
        mid = q_ref.shape[0] // 2
        q_ref[:mid] = q_refs[0][:mid]
        q_ref[mid:] = q_refs[1][mid:]
    token[...] = jnp.zeros_like(token)
    blocks, brow, hd = q_ref.shape
    roll, slots = k_ref.shape[0], k_ref.shape[1]
    nb = XL * NZ // roll
    nblk = nb * roll
    held = 0 if blocks == nblk else span[0]
    rows = nb * brow
    tok = nk_ref.shape[0]
    small = [
        pltpu.make_async_copy(cl_hbm, cl_ref, sems.at[0]),
        pltpu.make_async_copy(tl_hbm, tl_ref, sems.at[1]),
    ]
    for c in small:
        c.start()
    for c in small:
        c.wait()
    y = lax.axis_index("y")
    ctx = (lax.axis_index("xl") * NZ + lax.axis_index("z")) * NY + y
    per_roll = nblk * NY // roll
    own = lax.div(ctx, per_roll)
    first = lax.rem(ctx, per_roll) * tok
    hop = hops[0] if two == 1 else jnp.where(own < roll // 2, hops[0], hops[1])
    off = lax.rem(y - hop + NY, NY) * tok
    lane = lax.broadcasted_iota(jnp.int32, (brow, hd), 1)

    n_roll = span[1] - span[0]
    slot_of = lax.broadcasted_iota(jnp.int32, (slots, hd), 0)
    per = sub // brow
    each = rows // sub

    def split(base, count):
        qf = q_ref[pl.ds(base, count)].reshape(count * brow, hd).astype(F32) * (hd**-0.5 * LOG2E)
        hi = qf.astype(BF)
        lo = (qf - hi.astype(F32)).astype(BF)
        return jnp.concatenate([hi, lo], axis=1)

    def seen_slots(r):
        return jnp.clip(cl_ref[r] - ctx * slots, 0, slots)

    def score(r, i):
        k = k_ref[r]
        k = jnp.where(slot_of < seen_slots(r), k, jnp.broadcast_to(k[:1], k.shape))
        return dot_t(split((r - held) * nb + i * per, per), jnp.concatenate([k, k], axis=1))

    def together(p, carry):
        steps = [(span[0] + 2 * p + x, i) for x in range(2) for i in range(each)]
        ahead = score(*steps[0])
        for x, (r, i) in enumerate(steps):
            s = ahead
            if x + 1 < len(steps):
                ahead = score(*steps[x + 1])
            m = jnp.max(s, axis=1, keepdims=True).astype(BF).astype(F32)
            p_ = jnp.exp2(s - m).astype(BF)
            v = v_ref[r]
            seen = slot_of < seen_slots(r)
            zero = jnp.zeros_like(v)
            vv = jnp.concatenate([jnp.where(seen, v, zero), jnp.where(seen, jnp.ones_like(v), zero)], axis=1)
            pv = jnp.dot(p_, vv, preferred_element_type=F32)
            at = (r - span[0], slice(i * sub, (i + 1) * sub))
            some = seen_slots(r) > 0
            n_s[at] = jnp.where(some, pv[:, :hd], 0.0)
            l_s[at] = jnp.where(some, pv[:, hd:], 0.0)
            m_s[at] = jnp.broadcast_to(jnp.where(some, m, FLOOR), (sub, hd))
        return carry

    lax.fori_loop(0, n_roll // 2, together, 0)

    @pl.when((own >= span[0]) & (own < span[1]))
    def _():
        pad = jnp.zeros((hd - tok, hd), F32)
        nk = jnp.concatenate([nk_ref[...].astype(F32), pad], axis=0).astype(BF)
        nv = jnp.concatenate([nv_ref[...].astype(F32), pad], axis=0).astype(BF)
        s = dot_t(split((own - held) * nb, nb), jnp.concatenate([nk, nk], axis=1))
        row = lax.broadcasted_iota(jnp.int32, s.shape, 0)
        col = lax.broadcasted_iota(jnp.int32, s.shape, 1)
        t = (row // brow) * (NY * tok) + off + row % tok
        j = first + col
        seen = (col < tok) & (j <= t) & (j < tl_ref[own])
        s = jnp.where(seen, s, FLOOR)
        at = own - span[0]
        mo = m_s[at]
        mn = jnp.maximum(mo, jnp.max(s, axis=1, keepdims=True)).astype(BF).astype(F32)
        a = jnp.exp2(mo - mn)
        p = jnp.where(seen, jnp.exp2(s - mn), 0.0).astype(BF)
        pv = jnp.dot(p, jnp.concatenate([nv, jnp.ones_like(nv)], axis=1), preferred_element_type=F32)
        n_s[at] = n_s[at] * a + pv[:, :hd]
        l_s[at] = l_s[at] * a + pv[:, hd:]
        m_s[at] = mn

    for half, o_ref in enumerate(outs):

        def emit(x, carry):
            for b in range(nb):
                at = (x + half * (n_roll // two), slice(b * brow, (b + 1) * brow))
                out = x * nb + b
                o_ref[out, :brow, :] = n_s[at].astype(BF)
                total = l_s[at]
                head = total.astype(BF).astype(F32)
                aux = jnp.where(lane == 0, m_s[at], jnp.where(lane == 1, head, total - head))
                o_ref[out, brow:, :] = aux.T[:AUX].astype(BF)
            return carry

        lax.fori_loop(0, n_roll // two, emit, 0)


def attend(hops, cl, tl, qs, k, v, nk, nv, after=(), span=None, sub=512):
    brow, hd = qs[0].shape[1:]
    roll, slots = k.shape[0], k.shape[1]
    span = span or (0, roll)
    nb = XL * NZ // roll
    rows = nb * brow
    n = span[1] - span[0]
    two = len(hops)
    part = jax.ShapeDtypeStruct((nb * n // two, brow + AUX, hd), BF)
    return pl.pallas_call(
        functools.partial(attend_kernel, hops, sub, span, len(after)),
        in_specs=[ANY, ANY] + [VM] * (4 + two) + [ANY] * len(after),
        out_specs=[VM] * (two + 1),
        out_shape=[part] * two + [jax.ShapeDtypeStruct((8, 128), F32)],
        scratch_shapes=[pltpu.SMEM((roll,), jnp.int32)] * 2
        + [pltpu.VMEM((n, rows, hd), F32)] * 3
        + [pltpu.SemaphoreType.DMA((2,))]
        + ([pltpu.VMEM(qs[0].shape, BF)] if two == 2 else []),
        compiler_params=pltpu.CompilerParams(vmem_limit_bytes=ATTEND_VMEM),
        cost_estimate=pl.CostEstimate(
            flops=8 * n * rows * slots * hd,
            bytes_accessed=4 * n * slots * hd,
            transcendentals=n * rows * slots,
        ),
        name="attend",
    )(cl, tl, k, v, nk, nv, *qs, *after)


def weights_of(auxs):
    tops = [a[0:1] for a in auxs]
    sums = [a[1:2] + a[2:3] for a in auxs]
    top = functools.reduce(jnp.maximum, tops)
    ws = [jnp.exp2(t - top) for t in tops]
    total = functools.reduce(jnp.add, [w * s for w, s in zip(ws, sums)])
    return top, ws, total


def columns(rows_list):
    n = len(rows_list)
    lanes = rows_list[0].shape[1]
    pad = jnp.zeros((lanes - n, lanes), F32)
    return jnp.concatenate(list(rows_list) + [pad], axis=0).T


def merge_kernel(passed, *refs):
    n_in = len(refs) - 1 - 2 * passed if passed else len(refs) - 1
    whole, halves = refs[0], refs[1 : n_in - passed]
    o_ref = refs[n_in]
    if passed:
        w_ref, first_ref, second_ref = refs[n_in - 1], refs[n_in + 1], refs[n_in + 2]
        half = first_ref.shape[0]
        first_ref[...] = w_ref[:half]
        second_ref[...] = w_ref[half:]
    nb, prow, lanes = o_ref.shape
    brow = prow - AUX
    cut = nb // 2
    for b in range(nb):
        side = b // cut
        parts = [(whole, b)] + [(p, b - side * cut) for p in halves[side::2]]
        top, ws, total = weights_of([p[i, brow:, :].astype(F32) for p, i in parts])
        cols = columns(ws)
        acc = 0.0
        for n, (p, i) in enumerate(parts):
            acc = acc + cols[:, n : n + 1] * p[i, :brow, :].astype(F32)
        o_ref[b, :brow, :] = acc.astype(BF)
        head = total.astype(BF).astype(F32)
        aux = jnp.concatenate([top, head, total - head, jnp.zeros((AUX - 3, lanes), F32)], axis=0)
        o_ref[b, brow:, :] = aux.astype(BF)


def merge(parts, w=None):
    out = [jax.ShapeDtypeStruct(parts[0].shape, BF)]
    given = list(parts)
    if w is not None:
        given.append(w)
        out += [jax.ShapeDtypeStruct((w.shape[0] // 2, w.shape[1]), w.dtype)] * 2
    return pl.pallas_call(
        functools.partial(merge_kernel, int(w is not None)),
        in_specs=[VM] * len(given),
        out_specs=[VM] * len(out),
        out_shape=out,
        compiler_params=pltpu.CompilerParams(vmem_limit_bytes=SMALL_VMEM),
        name="merge",
    )(*given)


def finish_kernel(tok, x_ref, *rest):
    o_ref = rest[-1]
    n, prow, _ = x_ref.shape
    brow = prow - AUX
    _, ws, total = weights_of([x_ref[i, brow:, :].astype(F32) for i in range(n)])
    inv = 1.0 / total
    cols = columns([w * inv for w in ws])
    acc = 0.0
    for i in range(n):
        acc = acc + cols[:, i : i + 1] * x_ref[i, :brow, :].astype(F32)
    rows = jnp.concatenate([acc[g * tok : (g + 1) * tok] for g in range(brow // tok)], axis=1)
    pair = jnp.concatenate([rows, rows], axis=0).astype(BF)
    step = 2 * tok
    for c in range(n // 2):
        o_ref[c * step : (c + 1) * step, :] = pair


def finish(x, tok, after):
    n, prow, hd = x.shape
    width = (prow - AUX) // tok * hd
    return pl.pallas_call(
        functools.partial(finish_kernel, tok),
        in_specs=[VM] + [ANY] * len(after),
        out_specs=VM,
        out_shape=jax.ShapeDtypeStruct((n * tok, width), BF),
        compiler_params=pltpu.CompilerParams(vmem_limit_bytes=SMALL_VMEM),
        name="finish",
    )(x, *after)


def project_kernel(a_ref, w_ref, *rest):
    o_ref = rest[-1]
    half = w_ref.shape[0] // 2
    y = lax.axis_index("y")
    pieces = [(w_ref.at[:half], w_ref.at[half:])] + [rest[2 * i : 2 * i + 2] for i in range(NY - 1)]
    for k, (top, low) in enumerate(pieces):
        out = jnp.dot(a_ref[:, :half], top[...], preferred_element_type=F32)
        out = out + jnp.dot(a_ref[:, half:], low[...], preferred_element_type=F32)
        o_ref[lax.rem(y - k + NY, NY)] = out.astype(BF)


def project(a, w, others):
    return pl.pallas_call(
        project_kernel,
        in_specs=[VM] * (2 + len(others)),
        out_specs=VM,
        out_shape=jax.ShapeDtypeStruct((NY, a.shape[0], w.shape[1]), BF),
        compiler_params=pltpu.CompilerParams(vmem_limit_bytes=SMALL_VMEM),
        name="project",
    )(a, w, *others)


def shift(x, k):
    return lax.ppermute(x, "y", [(i, (i + k) % NY) for i in range(NY)])


def on_device(queries, new_keys, new_values, cache_keys, cache_values, out_weight, context_lengths, turn_lengths):
    tok, q_width = queries.shape
    hd = cache_keys.shape[3]
    groups = q_width // hd
    roll = cache_keys.shape[1]
    blocks = XL * NZ
    brow = groups * tok
    plane = ("xl", "z")

    rows = queries.reshape(tok, groups, hd).transpose(1, 0, 2).reshape(1, brow, hd)
    half = q_width // 2
    up1, low3 = shift(out_weight[:half], 1), shift(out_weight[half:], 3)
    q0 = lax.all_to_all(jnp.broadcast_to(rows, (blocks, brow, hd)), plane, 0, 0, tiled=True)
    near = {k: shift(q0, k) for k in (1, 3)}
    cut = blocks // 2
    far = (shift(near[1][:cut], 1), shift(near[3][cut:], 3))
    lens = (context_lengths, turn_lengths)
    kv = prepare(cache_keys[0], cache_values[0], new_keys, new_values)

    own, token = attend((0,), *lens, (q0,), *kv, after=(up1, low3))

    def away(hops, qs, span=None, after=()):
        *parts, _ = attend(hops, *lens, qs, *kv, after=(token,) + after, span=span)
        return [shift(p, -k) for p, k in zip(parts, hops)]

    (hi2,) = away((2,), far[1:], (roll // 2, roll))
    lo1, hi3 = away((1, 3), (near[1], near[3]))
    lo3, hi1 = away((3, 1), (near[3], near[1]), after=far)
    (lo2,) = away((2,), far[:1], (0, roll // 2))
    (early,) = merge([own, lo1, hi1, lo3, hi3])
    merged, top, low = merge([early, lo2, hi2], out_weight)

    up3, low1 = shift(top, 3), shift(low, 1)
    gathered = lax.all_to_all(merged, plane, 0, 0, tiled=True)
    copies = finish(gathered, tok, (up3, low1))
    up2, low2 = shift(up1, 1), shift(low3, 3)
    attended = lax.all_to_all(copies, plane, 0, 0, tiled=True).reshape(blocks * tok, q_width)
    width = out_weight.shape[1]
    rb = blocks * tok // roll
    mine = project(attended, out_weight, (up1, low1, up2, low2, up3, low3))
    got = lax.all_to_all(mine.reshape(NY * roll, rb, width), ("y",) + HEAD, 0, 0, tiled=True)
    total = jnp.sum(got.reshape(NY, roll, rb // tok, tok, width).astype(F32), axis=1)
    return total.astype(BF).transpose(1, 0, 2, 3).reshape(NY * rb, width)


def solution(mesh):
    fine = Mesh(mesh.devices.reshape(XL, NZ, NY, XH, CORE), ("xl", "z", "y", "xh", "core"))
    in_specs = (
        P(CTX, HEAD),
        P(CTX, HEAD),
        P(CTX, HEAD),
        P(HEAD, None, CTX, None),
        P(HEAD, None, CTX, None),
        P(HEAD, CTX),
        P(),
        P(),
    )
    return jax.shard_map(
        on_device, mesh=fine, in_specs=in_specs, out_specs=P(HEAD, CTX), check_vma=False
    )
```

```python
import functools

import jax
import jax.numpy as jnp
from jax import lax
from jax.experimental import pallas as pl
from jax.experimental.pallas import tpu as pltpu
from jax.sharding import Mesh
from jax.sharding import PartitionSpec as P

FLOOR = -(2.0**99)
LOG2E = 1.4426950408889634
BF = jnp.bfloat16
F32 = jnp.float32
AUX = 16
XL, NZ, NY, XH, CORE = 2, 8, 4, 2, 2
VM = pl.BlockSpec(memory_space=pltpu.VMEM)
ANY = pl.BlockSpec(memory_space=pl.ANY)
CTX = ("xl", "z", "y")
HEAD = ("xh", "core")
ATTEND_VMEM = 36 * 2**20
SMALL_VMEM = 16 * 2**20
LATE = 5


def dot_t(a, b):
    return lax.dot_general(a, b, (((1,), (1,)), ((), ())), preferred_element_type=F32)


def prepare_kernel(k_in, v_in, nk_in, nv_in, k_out, v_out, nk_out, nv_out, sems):
    pairs = ((k_in, k_out), (v_in, v_out), (nk_in, nk_out), (nv_in, nv_out))
    copies = [pltpu.make_async_copy(a, b, sems.at[i]) for i, (a, b) in enumerate(pairs)]
    for c in copies:
        c.start()
    for c in copies:
        c.wait()


def prepare(*given):
    return pl.pallas_call(
        prepare_kernel,
        in_specs=[ANY] * len(given),
        out_specs=[VM] * len(given),
        out_shape=[jax.ShapeDtypeStruct(a.shape, a.dtype) for a in given],
        scratch_shapes=[pltpu.SemaphoreType.DMA((len(given),))],
        compiler_params=pltpu.CompilerParams(vmem_limit_bytes=SMALL_VMEM),
        name="prepare",
    )(*given)


def attend_kernel(hops, sub, span, n_after, cl_hbm, tl_hbm, k_ref, v_ref, nk_ref, nv_ref, *rest):
    two = len(hops)
    q_refs, outs = rest[:two], rest[two + n_after : two + n_after + two]
    token, cl_ref, tl_ref, n_s, l_s, m_s, sems = rest[two + n_after + two : two + n_after + two + 7]
    q_ref = q_refs[0]
    if two == 2:
        q_ref = rest[-1]
        mid = q_ref.shape[0] // 2
        q_ref[:mid] = q_refs[0][:mid]
        q_ref[mid:] = q_refs[1][mid:]
    token[...] = jnp.zeros_like(token)
    blocks, brow, hd = q_ref.shape
    roll, slots = k_ref.shape[0], k_ref.shape[1]
    nb = XL * NZ // roll
    nblk = nb * roll
    held = 0 if blocks == nblk else span[0]
    rows = nb * brow
    tok = nk_ref.shape[0]
    small = [
        pltpu.make_async_copy(cl_hbm, cl_ref, sems.at[0]),
        pltpu.make_async_copy(tl_hbm, tl_ref, sems.at[1]),
    ]
    for c in small:
        c.start()
    for c in small:
        c.wait()
    y = lax.axis_index("y")
    ctx = (lax.axis_index("xl") * NZ + lax.axis_index("z")) * NY + y
    per_roll = nblk * NY // roll
    own = lax.div(ctx, per_roll)
    first = lax.rem(ctx, per_roll) * tok
    hop = hops[0] if two == 1 else jnp.where(own < roll // 2, hops[0], hops[1])
    off = lax.rem(y - hop + NY, NY) * tok
    lane = lax.broadcasted_iota(jnp.int32, (brow, hd), 1)

    n_roll = span[1] - span[0]
    slot_of = lax.broadcasted_iota(jnp.int32, (slots, hd), 0)
    per = sub // brow
    each = rows // sub

    def split(base, count):
        qf = q_ref[pl.ds(base, count)].reshape(count * brow, hd).astype(F32) * (hd**-0.5 * LOG2E)
        hi = qf.astype(BF)
        lo = (qf - hi.astype(F32)).astype(BF)
        return jnp.concatenate([hi, lo], axis=1)

    def seen_slots(r):
        return jnp.clip(cl_ref[r] - ctx * slots, 0, slots)

    def score(r, i):
        k = k_ref[r]
        k = jnp.where(slot_of < seen_slots(r), k, jnp.broadcast_to(k[:1], k.shape))
        return dot_t(split((r - held) * nb + i * per, per), jnp.concatenate([k, k], axis=1))

    def together(p, carry):
        steps = [(span[0] + 2 * p + x, i) for x in range(2) for i in range(each)]
        ahead = score(*steps[0])
        for x, (r, i) in enumerate(steps):
            s = ahead
            if x + 1 < len(steps):
                ahead = score(*steps[x + 1])
            m = jnp.max(s, axis=1, keepdims=True).astype(BF).astype(F32)
            p_ = jnp.exp2(s - m).astype(BF)
            v = v_ref[r]
            seen = slot_of < seen_slots(r)
            zero = jnp.zeros_like(v)
            vv = jnp.concatenate([jnp.where(seen, v, zero), jnp.where(seen, jnp.ones_like(v), zero)], axis=1)
            pv = jnp.dot(p_, vv, preferred_element_type=F32)
            at = (r - span[0], slice(i * sub, (i + 1) * sub))
            some = seen_slots(r) > 0
            n_s[at] = jnp.where(some, pv[:, :hd], 0.0)
            l_s[at] = jnp.where(some, pv[:, hd:], 0.0)
            m_s[at] = jnp.broadcast_to(jnp.where(some, m, FLOOR), (sub, hd))
        return carry

    lax.fori_loop(0, n_roll // 2, together, 0)

    @pl.when((own >= span[0]) & (own < span[1]))
    def _():
        pad = jnp.zeros((hd - tok, hd), F32)
        nk = jnp.concatenate([nk_ref[...].astype(F32), pad], axis=0).astype(BF)
        nv = jnp.concatenate([nv_ref[...].astype(F32), pad], axis=0).astype(BF)
        s = dot_t(split((own - held) * nb, nb), jnp.concatenate([nk, nk], axis=1))
        row = lax.broadcasted_iota(jnp.int32, s.shape, 0)
        col = lax.broadcasted_iota(jnp.int32, s.shape, 1)
        t = (row // brow) * (NY * tok) + off + row % tok
        j = first + col
        seen = (col < tok) & (j <= t) & (j < tl_ref[own])
        s = jnp.where(seen, s, FLOOR)
        at = own - span[0]
        mo = m_s[at]
        mn = jnp.maximum(mo, jnp.max(s, axis=1, keepdims=True)).astype(BF).astype(F32)
        a = jnp.exp2(mo - mn)
        p = jnp.where(seen, jnp.exp2(s - mn), 0.0).astype(BF)
        pv = jnp.dot(p, jnp.concatenate([nv, jnp.ones_like(nv)], axis=1), preferred_element_type=F32)
        n_s[at] = n_s[at] * a + pv[:, :hd]
        l_s[at] = l_s[at] * a + pv[:, hd:]
        m_s[at] = mn

    for half, o_ref in enumerate(outs):

        def emit(x, carry):
            for b in range(nb):
                at = (x + half * (n_roll // two), slice(b * brow, (b + 1) * brow))
                out = x * nb + b
                o_ref[out, :brow, :] = n_s[at].astype(BF)
                total = l_s[at]
                head = total.astype(BF).astype(F32)
                aux = jnp.where(lane == 0, m_s[at], jnp.where(lane == 1, head, total - head))
                o_ref[out, brow:, :] = aux.T[:AUX].astype(BF)
            return carry

        lax.fori_loop(0, n_roll // two, emit, 0)


def attend(hops, cl, tl, qs, k, v, nk, nv, after=(), span=None, sub=512):
    brow, hd = qs[0].shape[1:]
    roll, slots = k.shape[0], k.shape[1]
    span = span or (0, roll)
    nb = XL * NZ // roll
    rows = nb * brow
    n = span[1] - span[0]
    two = len(hops)
    part = jax.ShapeDtypeStruct((nb * n // two, brow + AUX, hd), BF)
    return pl.pallas_call(
        functools.partial(attend_kernel, hops, sub, span, len(after)),
        in_specs=[ANY, ANY] + [VM] * (4 + two) + [ANY] * len(after),
        out_specs=[VM] * (two + 1),
        out_shape=[part] * two + [jax.ShapeDtypeStruct((8, 128), F32)],
        scratch_shapes=[pltpu.SMEM((roll,), jnp.int32)] * 2
        + [pltpu.VMEM((n, rows, hd), F32)] * 3
        + [pltpu.SemaphoreType.DMA((2,))]
        + ([pltpu.VMEM(qs[0].shape, BF)] if two == 2 else []),
        compiler_params=pltpu.CompilerParams(vmem_limit_bytes=ATTEND_VMEM),
        cost_estimate=pl.CostEstimate(
            flops=8 * n * rows * slots * hd,
            bytes_accessed=4 * n * slots * hd,
            transcendentals=n * rows * slots,
        ),
        name="attend",
    )(cl, tl, k, v, nk, nv, *qs, *after)


def weights_of(auxs):
    tops = [a[0:1] for a in auxs]
    sums = [a[1:2] + a[2:3] for a in auxs]
    top = functools.reduce(jnp.maximum, tops)
    ws = [jnp.exp2(t - top) for t in tops]
    total = functools.reduce(jnp.add, [w * s for w, s in zip(ws, sums)])
    return top, ws, total


def columns(rows_list):
    n = len(rows_list)
    lanes = rows_list[0].shape[1]
    pad = jnp.zeros((lanes - n, lanes), F32)
    return jnp.concatenate(list(rows_list) + [pad], axis=0).T


def merge_kernel(passed, *refs):
    n_in = len(refs) - 1 - 2 * passed if passed else len(refs) - 1
    whole, halves = refs[0], refs[1 : n_in - passed]
    o_ref = refs[n_in]
    if passed:
        w_ref, first_ref, second_ref = refs[n_in - 1], refs[n_in + 1], refs[n_in + 2]
        half = first_ref.shape[0]
        first_ref[...] = w_ref[:half]
        second_ref[...] = w_ref[half:]
    nb, prow, lanes = o_ref.shape
    brow = prow - AUX
    cut = nb // 2
    for b in range(nb):
        side = b // cut
        parts = [(whole, b)] + [(p, b - side * cut) for p in halves[side::2]]
        top, ws, total = weights_of([p[i, brow:, :].astype(F32) for p, i in parts])
        cols = columns(ws)
        acc = 0.0
        for n, (p, i) in enumerate(parts):
            acc = acc + cols[:, n : n + 1] * p[i, :brow, :].astype(F32)
        o_ref[b, :brow, :] = acc.astype(BF)
        head = total.astype(BF).astype(F32)
        aux = jnp.concatenate([top, head, total - head, jnp.zeros((AUX - 3, lanes), F32)], axis=0)
        o_ref[b, brow:, :] = aux.astype(BF)


def merge(parts, w=None):
    out = [jax.ShapeDtypeStruct(parts[0].shape, BF)]
    given = list(parts)
    if w is not None:
        given.append(w)
        out += [jax.ShapeDtypeStruct((w.shape[0] // 2, w.shape[1]), w.dtype)] * 2
    return pl.pallas_call(
        functools.partial(merge_kernel, int(w is not None)),
        in_specs=[VM] * len(given),
        out_specs=[VM] * len(out),
        out_shape=out,
        compiler_params=pltpu.CompilerParams(vmem_limit_bytes=SMALL_VMEM),
        name="merge",
    )(*given)


def finish_kernel(tok, x_ref, *rest):
    o_ref = rest[-1]
    n, prow, _ = x_ref.shape
    brow = prow - AUX
    _, ws, total = weights_of([x_ref[i, brow:, :].astype(F32) for i in range(n)])
    inv = 1.0 / total
    cols = columns([w * inv for w in ws])
    acc = 0.0
    for i in range(n):
        acc = acc + cols[:, i : i + 1] * x_ref[i, :brow, :].astype(F32)
    rows = jnp.concatenate([acc[g * tok : (g + 1) * tok] for g in range(brow // tok)], axis=1)
    pair = jnp.concatenate([rows, rows], axis=0).astype(BF)
    step = 2 * tok
    for c in range(n // 2):
        o_ref[c * step : (c + 1) * step, :] = pair


def finish(x, tok, after):
    n, prow, hd = x.shape
    width = (prow - AUX) // tok * hd
    return pl.pallas_call(
        functools.partial(finish_kernel, tok),
        in_specs=[VM] + [ANY] * len(after),
        out_specs=VM,
        out_shape=jax.ShapeDtypeStruct((n * tok, width), BF),
        compiler_params=pltpu.CompilerParams(vmem_limit_bytes=SMALL_VMEM),
        name="finish",
    )(x, *after)


def project_kernel(a_ref, *rest):
    *pieces, o_ref, late, sem = rest
    fetch = pltpu.make_async_copy(pieces[LATE], late, sem)
    fetch.start()
    half = late.shape[0]
    y = lax.axis_index("y")
    for k in (0, 1, 3, 2):
        top, low = pieces[2 * k : 2 * k + 2]
        if 2 * k + 1 == LATE:
            fetch.wait()
            low = late
        out = jnp.dot(a_ref[:, :half], top[...], preferred_element_type=F32)
        out = out + jnp.dot(a_ref[:, half:], low[...], preferred_element_type=F32)
        o_ref[lax.rem(y - k + NY, NY)] = out.astype(BF)


def project(a, pieces):
    return pl.pallas_call(
        project_kernel,
        in_specs=[VM] + [ANY if i == LATE else VM for i in range(len(pieces))],
        out_specs=VM,
        out_shape=jax.ShapeDtypeStruct((NY, a.shape[0], pieces[0].shape[1]), BF),
        scratch_shapes=[pltpu.VMEM(pieces[LATE].shape, BF), pltpu.SemaphoreType.DMA(())],
        compiler_params=pltpu.CompilerParams(vmem_limit_bytes=SMALL_VMEM),
        name="project",
    )(a, *pieces)


def shift(x, k):
    return lax.ppermute(x, "y", [(i, (i + k) % NY) for i in range(NY)])


def on_device(queries, new_keys, new_values, cache_keys, cache_values, out_weight, context_lengths, turn_lengths):
    tok, q_width = queries.shape
    hd = cache_keys.shape[3]
    groups = q_width // hd
    roll = cache_keys.shape[1]
    blocks = XL * NZ
    brow = groups * tok
    plane = ("xl", "z")

    rows = queries.reshape(tok, groups, hd).transpose(1, 0, 2).reshape(1, brow, hd)
    half = q_width // 2
    up1, low3 = shift(out_weight[:half], 1), shift(out_weight[half:], 3)
    q0 = lax.all_to_all(jnp.broadcast_to(rows, (blocks, brow, hd)), plane, 0, 0, tiled=True)
    near = {k: shift(q0, k) for k in (1, 3)}
    cut = blocks // 2
    far = (shift(near[1][:cut], 1), shift(near[3][cut:], 3))
    lens = (context_lengths, turn_lengths)
    kv = prepare(cache_keys[0], cache_values[0], new_keys, new_values)

    own, token = attend((0,), *lens, (q0,), *kv, after=(up1, low3))

    def away(hops, qs, span=None, after=()):
        *parts, _ = attend(hops, *lens, qs, *kv, after=(token,) + after, span=span)
        return [shift(p, -k) for p, k in zip(parts, hops)]

    (hi2,) = away((2,), far[1:], (roll // 2, roll))
    lo1, hi3 = away((1, 3), (near[1], near[3]))
    lo3, hi1 = away((3, 1), (near[3], near[1]), after=far)
    (lo2,) = away((2,), far[:1], (0, roll // 2))
    (early,) = merge([own, lo1, hi1, lo3, hi3])
    merged, top, low = merge([early, lo2, hi2], out_weight)

    up3, low1 = shift(top, 3), shift(low, 1)
    gathered = lax.all_to_all(merged, plane, 0, 0, tiled=True)
    copies = finish(gathered, tok, (up3, low1))
    up2, low2 = shift(up1, 1), shift(low3, 3)
    attended = lax.all_to_all(copies, plane, 0, 0, tiled=True).reshape(blocks * tok, q_width)
    width = out_weight.shape[1]
    rb = blocks * tok // roll
    mine = project(attended, (top, low, up1, low1, up2, low2, up3, low3))
    got = lax.all_to_all(mine.reshape(NY * roll, rb, width), ("y",) + HEAD, 0, 0, tiled=True)
    total = jnp.sum(got.reshape(NY, roll, rb // tok, tok, width).astype(F32), axis=1)
    return total.astype(BF).transpose(1, 0, 2, 3).reshape(NY * rb, width)


def solution(mesh):
    fine = Mesh(mesh.devices.reshape(XL, NZ, NY, XH, CORE), ("xl", "z", "y", "xh", "core"))
    in_specs = (
        P(CTX, HEAD),
        P(CTX, HEAD),
        P(CTX, HEAD),
        P(HEAD, None, CTX, None),
        P(HEAD, None, CTX, None),
        P(HEAD, CTX),
        P(),
        P(),
    )
    return jax.shard_map(
        on_device, mesh=fine, in_specs=in_specs, out_specs=P(HEAD, CTX), check_vma=False
    )
```
